256 devices in a mesh: dp: 4 (over z_hi), expert: 64 (over z_lo, y, x, core).
Axes of the slice: x: 4, y: 4, z: 8 (z_hi: 4, z_lo: 2; z = z_hi * 2 + z_lo), core: 2. Of those that a mesh axis runs over, the one named last changes fastest.
Arguments:
- grad_out: bfloat16 [40960, 3584], P(('dp', 'expert')), may hold values from -1.5 to 1.5
- routes: int32 [40960, 2], P(('dp', 'expert')), may hold values from 0 to 63, all different within a row; in each aligned block of 160 rows (0 to 159, 160 to 319, ...) at most 10 rows name the same one
- route_weight: bfloat16 [40960, 2], P(('dp', 'expert')), may hold values from 0.099609375 to 1
- hidden_saved: bfloat16 [64, 4, 64, 10, 1024], P('expert', 'dp'), may hold values from -6 to 6
- down_weight: bfloat16 [64, 1024, 3584], P('expert', 'dp'), may hold values from -0.1875 to 0.1875
Outputs:
- down_grad: float32 [64, 1024, 3584], P('expert', 'dp')
- hidden_grad: bfloat16 [64, 4, 64, 10, 1024], P('expert', 'dp')
- prob_grad: float32 [40960, 2], P(('dp', 'expert'))
The draws below stay inside these ranges and needn't reach their ends.
Inputs may be any that keep to these rules, and one draw needn't show every extreme that they name: `routes`: each row names 2 different experts; among the rows of one device no expert is named by more than 10 rows, a bound that some block reaches; every expert is named somewhere.
All inputs are finite; a program needn't handle non-finite values.
Results may differ from the reference program's by a relative error of at most 0.014.
Values may be sent and summed in bfloat16 or wider, within the bound.
A program may use at most 128 MiB of HBM per device.

```python
import math
import jax
import jax.numpy as jnp
import numpy as np
from jax import lax

D = 3584
H = 1024
TOK_DEV = 160
ROUTES = 2
EXPERTS = 64
GROUPS = 4
CAP = 10
TOKENS = 40960


def level_of(own_key, shape, cuts, smallest, high):
    level, own = 1.0, jax.random.fold_in(own_key, 6)
    for dim, shards_of in cuts:
        draws = jnp.exp(jax.random.uniform(jax.random.fold_in(own, dim), (shards_of,), jnp.float32, smallest / len(cuts), high / len(cuts)))
        level = level * jnp.repeat(draws, shape[dim] // shards_of).reshape([-1 if axis == dim else 1 for axis in range(len(shape))])
    return level


def assign_block(own_key, own, number, rows, number_of, top, most, slope):
    sequence = jax.random.permutation(own_key, number_of)
    packed, usual = portions_of(number_of, rows * top, most, slope, True), portions_of(number_of, rows * top, most, slope, False)
    places = jnp.arange(number_of)

    def named(tallies, rotation):
        used = int((tallies > 0).sum())
        fixed = max(1, used // 4)
        passed = fixed + (places - fixed + rotation * (used - fixed)) % max(1, number_of - fixed)
        return jnp.zeros((number_of,), jnp.int32).at[sequence[jnp.where(places < fixed, places, passed)]].set(jnp.asarray(tallies, jnp.int32))

    tallies = jnp.where(number % 4 == 0, named(packed, number // 4), named(usual, number - number // 4 - 1))
    mixed = jax.random.permutation(jax.random.fold_in(own, 3), number_of)
    source_of, sink = mixed[0:number_of // 2 * 2:2], mixed[1:number_of // 2 * 2:2]
    margin = jnp.minimum(tallies[source_of] - 1, most - tallies[sink]) // 2
    margin = jnp.where((source_of == sequence[0]) | (sink == sequence[0]) | (tallies[sink] == 0), 0, jnp.maximum(margin, 0))
    passed = jax.random.randint(jax.random.fold_in(own, 4), (number_of // 2,), 0, 1 << 20) % (margin + 1)
    tallies = tallies.at[source_of].add(-passed).at[sink].add(passed)
    labels = jnp.searchsorted(jnp.cumsum(tallies), jnp.arange(rows * top), side="right").astype(jnp.int32)
    listing = labels.reshape(top, rows).T
    listing = listing[jax.random.permutation(jax.random.fold_in(own, 1), rows)]
    rotation = jax.random.randint(jax.random.fold_in(own, 2), (rows, 1), 0, top)
    return jnp.take_along_axis(listing, (jnp.arange(top)[None, :] + rotation) % top, axis=1)


def portions_of(amount, total, most, lean, full):
    weights = [(1 << 20) // math.isqrt(rank ** lean) + 1 for rank in range(1, amount + 1)]
    largest = most if full else min(most, max(-(-total // amount), total * weights[0] // sum(weights)))
    least = 1 if total - largest >= amount - 1 else 0
    counts, rest = [largest] + [least] * (amount - 1), total - largest - least * (amount - 1)
    while rest > 0:
        free = [i for i in range(1, amount) if counts[i] < largest] or [i for i in range(1, amount) if counts[i] < most]
        whole, budget = sum([weights[i] for i in free]), rest
        for i in free:
            addition = min(most - counts[i], max(1, budget * weights[i] // whole), rest)
            counts[i] = counts[i] + addition
            rest = rest - addition
    return np.array(counts)


def bell_draw(rng, extent, deviation, bound, split=(), kind=jnp.bfloat16):
    drawn = jax.random.normal(rng, extent, jnp.float32) * deviation
    if len(split) > 0:
        drawn = level_of(rng, extent, split, -0.22, 0.18) * drawn
    return jnp.clip(drawn, min=-bound, max=bound).astype(kind)


def setup_inputs(seed: int = 0) -> dict:
    streams_of = jax.random.split(jax.random.key(seed), 6)
    grad_out = bell_draw(streams_of[0], (TOKENS, D), 0.25, 1.5, ((0, 256),))
    routes_keys = jax.random.split(jax.random.fold_in(streams_of[1], 1), TOKENS // TOK_DEV)
    routes_turns = jax.random.permutation(jax.random.fold_in(streams_of[1], 3), TOKENS // TOK_DEV)
    routes = jax.vmap(lambda own, number: assign_block(jax.random.fold_in(streams_of[1], 2), own, number, TOK_DEV, EXPERTS, ROUTES, CAP, 1))(routes_keys, routes_turns).reshape((TOKENS, ROUTES))
    route_weight = jnp.clip(jnp.exp(math.log(1.0) - 2.306499 * jax.random.uniform(streams_of[2], (TOKENS, ROUTES), jnp.float32) ** level_of(streams_of[2], (TOKENS, ROUTES), ((0, 256),), -0.2, 0.2)), 0.099609375, 1.0).astype(jnp.bfloat16)
    hidden_saved = bell_draw(streams_of[3], (EXPERTS, GROUPS, EXPERTS, CAP, H), 1.0, 6.0, ((0, 64), (1, 4)))
    down_weight = bell_draw(streams_of[4], (EXPERTS, H, D), H ** -0.5, 0.1875, ((0, 64), (1, 4)))
    return dict(grad_out=grad_out, routes=routes, route_weight=route_weight, hidden_saved=hidden_saved, down_weight=down_weight)


def expert_step(operands):
    row_block, weight_block, hidden_block, down_block = operands
    row_block = row_block.reshape(-1, D)
    weight_block = weight_block.reshape(-1, 1).astype(jnp.float32)
    hidden_block = hidden_block.reshape(-1, H)
    expert_output = jnp.dot(hidden_block, down_block, preferred_element_type=jnp.float32)
    slot_prob = jnp.sum(row_block.astype(jnp.float32) * expert_output, axis=1)
    scaled = (weight_block * row_block.astype(jnp.float32)).astype(jnp.bfloat16)
    hidden_grad = jnp.dot(scaled, down_block.T, preferred_element_type=jnp.float32).astype(jnp.bfloat16)
    down_grad = jnp.dot(hidden_block.T, scaled, preferred_element_type=jnp.float32)
    return down_grad, hidden_grad, slot_prob


def reference(grad_out, routes, route_weight, hidden_saved, down_weight):
    flat_routes = routes.reshape(GROUPS, EXPERTS, TOK_DEV * ROUTES).astype(jnp.int32)
    member = (flat_routes[..., None] == jnp.arange(EXPERTS, dtype=jnp.int32)).astype(jnp.int32)
    earlier = jnp.cumsum(member, axis=2) - member
    slot_index = jnp.sum(earlier * member, axis=3).astype(jnp.int32)
    group_index = jnp.arange(GROUPS, dtype=jnp.int32)[:, None, None]
    source_index = jnp.arange(EXPERTS, dtype=jnp.int32)[None, :, None]
    token_index = (jnp.arange(TOK_DEV * ROUTES, dtype=jnp.int32) // ROUTES)[None, None, :]
    token_rows = grad_out.reshape(GROUPS, EXPERTS, TOK_DEV, D)
    picked = token_rows[group_index, source_index, token_index]
    sent_rows = jnp.zeros((EXPERTS, GROUPS, EXPERTS, CAP, D), jnp.bfloat16)
    sent_rows = sent_rows.at[flat_routes, group_index, source_index, slot_index].set(picked)
    weight_flat = route_weight.reshape(GROUPS, EXPERTS, TOK_DEV * ROUTES)
    sent_weights = jnp.zeros((EXPERTS, GROUPS, EXPERTS, CAP), jnp.bfloat16)
    sent_weights = sent_weights.at[flat_routes, group_index, source_index, slot_index].set(weight_flat)
    down_grad, hidden_grad, slot_prob = lax.map(expert_step, (sent_rows, sent_weights, hidden_saved, down_weight))
    slot_prob = slot_prob.reshape(EXPERTS, GROUPS, EXPERTS, CAP)
    prob_grad = slot_prob[flat_routes, group_index, source_index, slot_index].reshape(TOKENS, ROUTES)
    return down_grad, hidden_grad.reshape(EXPERTS, GROUPS, EXPERTS, CAP, H), prob_grad
```

```python
import functools

import jax
import jax.numpy as jnp
from jax import lax
from jax.experimental import pallas as pl
from jax.experimental.pallas import tpu as pltpu
from jax.sharding import PartitionSpec as P

MESH = pl.DeviceIdType.MESH
F32 = jnp.float32
BF16 = jnp.bfloat16
WIDE = 24
LANES = 128


def iota(shape, dim):
    return lax.broadcasted_iota(jnp.int32, shape, dim)


def kernel(
    n, cap, tokens, chunk, chunks, quarter,
    grad_ref, routes_ref, gate_ref, hidden_ref, weight_ref,
    own_ref, other_ref, hg_ref, prob_ref,
    tok, meta, onehot_t0, onehot_t1, onehot, send0, recv0, send, recv,
    wbuf, hid_all, hid_part, hid_rows, hid_t, q,
    dg_own, dg_send, hg_own, hg_send, part_out, part_in, back_out, back_in,
    load_sem, tok_ssem, tok_rsem, meta_ssem, meta_rsem, hid_ssem, hid_rsem,
    w_ssem, w_rsem, row_ssem, row_rsem, dg_ssem, dg_rsem, out_sem,
    hg_ssem, hg_rsem, part_ssem, part_rsem, back_ssem, back_rsem,
):
    d, e = lax.axis_index("dp"), lax.axis_index("expert")
    zl, i = e // n, e % n
    across = (1 - zl) * n + i
    da = 3 - d
    hq = d % 2
    db = d + 1 - 2 * hq
    hh = d // 2
    half = 2 * quarter
    span = 2 * WIDE
    rows = n * span
    slots = 2 * n * cap
    mine = pl.multiple_of(i * span, span)

    def remote(src, dst, ssem, rsem, device):
        return pltpu.make_async_remote_copy(
            src_ref=src, dst_ref=dst, send_sem=ssem, recv_sem=rsem,
            device_id=device, device_id_type=MESH,
        )

    def columns(k):
        return pl.ds(k * chunk, chunk)

    own_block = pl.multiple_of(zl * tokens, tokens)
    own_rows = pl.multiple_of(hq * quarter, quarter)
    tok_loads = [
        pltpu.make_async_copy(
            grad_ref.at[:, columns(k)], tok.at[k, pl.ds(own_block, tokens)], load_sem.at[k]
        )
        for k in range(chunks)
    ]
    w_loads = [
        pltpu.make_async_copy(
            weight_ref.at[:, columns(k)], wbuf.at[k, pl.ds(own_rows, quarter)], load_sem.at[chunks + k]
        )
        for k in range(chunks)
    ]
    hid_load = pltpu.make_async_copy(hidden_ref, hid_all, load_sem.at[2 * chunks])
    for load in tok_loads + [hid_load] + w_loads:
        load.start()

    barrier = pltpu.get_barrier_semaphore()

    def greet(j, carry):
        pl.semaphore_signal(
            barrier, inc=1, device_id=(d, (e + j) % (2 * n)), device_id_type=MESH
        )
        return carry

    lax.fori_loop(1, 2 * n, greet, 0)
    for device in ((da, e), (da, across), (db, e)):
        pl.semaphore_signal(barrier, inc=1, device_id=device, device_id_type=MESH)
    pl.semaphore_wait(barrier, 2 * n + 2)

    def token_copies(k):
        here = tok.at[k, pl.ds(own_block, tokens)]
        there = tok.at[k, pl.ds(pl.multiple_of((2 + zl) * tokens, tokens), tokens)]
        return [
            remote(here, here, tok_ssem.at[k, 0], tok_rsem.at[k, 0], (d, across)),
            remote(here, there, tok_ssem.at[k, 1], tok_rsem.at[k, 1], (da, e)),
            remote(here, there, tok_ssem.at[k, 2], tok_rsem.at[k, 2], (da, across)),
        ]

    def send_tokens(k):
        tok_loads[k].wait()
        for copy in token_copies(k):
            copy.start()

    send_tokens(0)

    experts = routes_ref[...]
    lane = iota((tokens, LANES), 1)
    name0, name1 = experts[:, 0:1], experts[:, 1:2]
    member0 = (lane == name0).astype(F32)
    member1 = (lane == name1).astype(F32)
    before = (iota((tokens, tokens), 1) < iota((tokens, tokens), 0)).astype(F32).astype(BF16)
    earlier = jnp.dot(before, (member0 + member1).astype(BF16), preferred_element_type=F32)
    slot0 = jnp.sum(earlier * member0, axis=1, keepdims=True)
    slot1 = jnp.sum(earlier * member1, axis=1, keepdims=True)
    gates = gate_ref[...].astype(F32)
    place0 = name0.astype(F32) * span + slot0
    place1 = name1.astype(F32) * span + slot1
    info = jnp.where(lane == 0, place0, 0.0)
    info = jnp.where(lane == 1, place1, info)
    info = jnp.where(lane == 2, gates[:, 0:1], info)
    info = jnp.where(lane == 3, gates[:, 1:2], info)
    meta[pl.ds(own_block, tokens), :] = info
    meta_here = meta.at[pl.ds(own_block, tokens)]
    meta_there = meta.at[pl.ds(pl.multiple_of((2 + zl) * tokens, tokens), tokens)]
    meta_copies = [
        remote(meta_here, meta_here, meta_ssem.at[0], meta_rsem.at[0], (d, across)),
        remote(meta_here, meta_there, meta_ssem.at[1], meta_rsem.at[1], (da, e)),
        remote(meta_here, meta_there, meta_ssem.at[2], meta_rsem.at[2], (da, across)),
    ]
    for copy in meta_copies:
        copy.start()
    send_tokens(1)

    hid_load.wait()
    hid_copy = remote(
        hid_all.at[:, pl.ds(pl.multiple_of((1 - hh) * half, half), half)],
        hid_part, hid_ssem, hid_rsem, (da, e),
    )
    hid_copy.start()
    for k in range(2, min(4, chunks)):
        send_tokens(k)

    for copy in meta_copies:
        copy.wait_recv()
    row_lane = iota((tokens, rows), 1).astype(F32)
    plane = (zl * rows).astype(F32)
    for block in range(4):
        part = pl.ds(block * tokens, tokens)
        offset = float((block // 2) * WIDE + (block % 2) * cap)
        seen = meta[part, :]
        onehot_t0[part, :] = (row_lane == seen[:, 0:1] - plane + offset).astype(F32).astype(BF16)
        onehot_t1[part, :] = (row_lane == seen[:, 1:2] - plane + offset).astype(F32).astype(BF16)

    tile = min(LANES, rows)

    def flip(t, carry):
        part = pl.ds(pl.multiple_of(t * tile, tile), tile)
        first = onehot_t0[:, part].T
        second = onehot_t1[:, part].T
        onehot[part, :] = first + second
        gate0 = jnp.broadcast_to(meta[:, 2:3], (4 * tokens, LANES)).astype(BF16)
        gate1 = jnp.broadcast_to(meta[:, 3:4], (4 * tokens, LANES)).astype(BF16)
        gate = jnp.dot(first, gate0, preferred_element_type=F32)
        gate = gate + jnp.dot(second, gate1, preferred_element_type=F32)
        send0[part, pl.ds(chunk, LANES)] = gate.astype(BF16)
        return carry

    lax.fori_loop(0, rows // tile, flip, 0)

    def buffers(k):
        return (send0, recv0) if k == 0 else (send.at[k - 1], recv.at[k - 1])

    pack = min(8, n)

    def gather(k):
        for copy in token_copies(k):
            copy.wait_recv()
        out, into = buffers(k)

        def step(s, carry):
            group = (i // pack + s) % (n // pack)
            part = pl.ds(pl.multiple_of(group * (pack * span), pack * span), pack * span)
            out[part, pl.ds(0, chunk)] = jnp.dot(
                onehot[part, :], tok[k], preferred_element_type=F32
            ).astype(BF16)

            def issue(j, inner):
                to = group * pack + (i + j) % pack

                @pl.when(to != i)
                def _():
                    remote(
                        out.at[pl.ds(pl.multiple_of(to * span, span), span)],
                        into.at[pl.ds(mine, span)],
                        row_ssem.at[k], row_rsem.at[k], (d, zl * n + to),
                    ).start()

                return inner

            return lax.fori_loop(0, pack, issue, carry)

        lax.fori_loop(0, n // pack, step, 0)
        into[pl.ds(mine, span), :] = out[pl.ds(mine, span), :]

    def row_wait(k):
        out, into = buffers(k)
        many = pl.ds(0, (n - 1) * span)
        return remote(out.at[many], into.at[many], row_ssem.at[k], row_rsem.at[k], (db, e))

    w_copies = [
        remote(
            wbuf.at[k, pl.ds(own_rows, quarter)], wbuf.at[k, pl.ds(own_rows, quarter)],
            w_ssem.at[k], w_rsem.at[k], (db, e),
        )
        for k in range(chunks)
    ]
    dg_copies = [
        remote(dg_send.at[k], other_ref.at[:, columns(k)], dg_ssem.at[k], dg_rsem.at[k], (db, e))
        for k in range(chunks)
    ]
    own_copies = [
        pltpu.make_async_copy(dg_own.at[k], own_ref.at[:, columns(k)], out_sem.at[k])
        for k in range(chunks)
    ]

    def order_hidden():
        hid_copy.wait_recv()
        at = iota((n * WIDE, slots), 1)
        source = at % (2 * n)
        target = (source % n) * WIDE + (source // n) * cap + at // (2 * n)
        order = (iota((n * WIDE, slots), 0) == target).astype(F32).astype(BF16)
        near = hid_all[:, pl.ds(pl.multiple_of(hh * half, half), half)]
        near = jnp.dot(order, near, preferred_element_type=F32).reshape(n, 1, WIDE, half)
        far = jnp.dot(order, hid_part[...], preferred_element_type=F32).reshape(n, 1, WIDE, half)
        both = jnp.concatenate([near, far], axis=1).reshape(rows, half)
        hid_rows[...] = both.astype(BF16)

    def weigh_hidden():
        def turn(t, carry):
            part = pl.ds(pl.multiple_of(t * tile, tile), tile)
            gate = recv0[part, pl.ds(chunk, LANES)].astype(F32)[:, 0:1]
            hid_t[:, part] = (hid_rows[part, :].astype(F32) * gate).astype(BF16).T
            return carry

        lax.fori_loop(0, rows // tile, turn, 0)

    def down(k):
        row_wait(k).wait_recv()
        if k == 0:
            weigh_hidden()
        into = buffers(k)[1]
        got = into[:, pl.ds(0, chunk)]
        theirs = pl.ds(pl.multiple_of((1 - hq) * quarter, quarter), quarter)
        dg_send[k] = jnp.dot(hid_t[theirs, :], got, preferred_element_type=F32).astype(BF16)
        dg_copies[k].start()
        dg_own[k] = jnp.dot(hid_t[pl.ds(own_rows, quarter), :], got, preferred_element_type=F32)
        own_copies[k].start()

    strip = rows // 6

    def project(k):
        w_copies[k].wait_recv()
        into = buffers(k)[1]

        def step(t, carry):
            part = pl.ds(pl.multiple_of(t * strip, strip), strip)
            more = lax.dot_general(
                into[part, pl.ds(0, chunk)], wbuf[k], (((1,), (1,)), ((), ())),
                preferred_element_type=F32,
            )
            q[part, :] = more if k == 0 else q[part, :] + more
            return carry

        lax.fori_loop(0, 6, step, 0)

    lag = min(3, chunks - 1)
    for k in range(chunks):
        gather(k)
        if k + 4 < chunks:
            send_tokens(k + 4)
        w_loads[k].wait()
        w_copies[k].start()
        if k == 0:
            order_hidden()
        if k >= 1:
            down(k - 1)
        if k >= 1 + lag:
            project(k - 1 - lag)
    down(chunks - 1)
    for k in range(chunks - 1 - lag, chunks):
        project(k)

    gate = recv0[:, pl.ds(chunk, LANES)].astype(F32)[:, 0:1]
    product = q[...]
    scaled = (product * gate).reshape(n, 2, WIDE, half)
    source = iota((slots, n * WIDE), 0)
    target = (source % n) * WIDE + (source % (2 * n)) // n * cap + source // (2 * n)
    order = (iota((slots, n * WIDE), 1) == target).astype(F32).astype(BF16)
    far = scaled[:, 1].reshape(n * WIDE, half).astype(BF16)
    hg_send[...] = jnp.dot(order, far, preferred_element_type=F32).astype(BF16)
    hg_columns = pl.ds(pl.multiple_of(hh * half, half), half)
    hg_copy = remote(hg_send, hg_ref.at[:, hg_columns], hg_ssem, hg_rsem, (da, e))
    hg_copy.start()
    sums = jnp.sum(hid_rows[...].astype(F32) * product, axis=1, keepdims=True)
    spread = jnp.where(
        iota((rows, LANES), 1) == iota((rows, LANES), 0) % WIDE, sums, 0.0
    ).reshape(n, 2, WIDE, LANES)
    spread = jnp.sum(spread, axis=2)
    part_out[...] = spread[:, 1]
    part_copy = remote(part_out, part_in, part_ssem, part_rsem, (da, e))
    part_copy.start()
    near = scaled[:, 0].reshape(n * WIDE, half).astype(BF16)
    hg_own[...] = jnp.dot(order, near, preferred_element_type=F32).astype(BF16)
    hg_store = pltpu.make_async_copy(hg_own, hg_ref.at[:, hg_columns], out_sem.at[chunks])
    hg_store.start()
    part_copy.wait_recv()
    total = spread[:, 0] + part_in[...]
    back_out[...] = jnp.broadcast_to(total[:, None, :], (n, 8, LANES))

    def give(j, carry):
        to = (e + j) % (2 * n)
        remote(
            back_out.at[to % n], back_in.at[e], back_ssem, back_rsem, (d, to)
        ).start()
        return carry

    lax.fori_loop(1, 2 * n, give, 0)
    back_in[e] = back_out[i]
    many = pl.ds(0, 2 * n - 1)
    remote(back_in.at[many], back_in.at[many], back_ssem, back_rsem, (db, e)).wait()
    table = back_in[...][:, 0, :]
    for k, (member, slot) in enumerate(((member0, slot0), (member1, slot1))):
        found = jnp.dot(
            member[:, : 2 * n], table, preferred_element_type=F32, precision=lax.Precision.HIGHEST
        )
        at = slot + (zl * cap).astype(F32)
        value = jnp.sum(jnp.where(lane.astype(F32) == at, found, 0.0), axis=1, keepdims=True)
        prob_ref[:, k : k + 1] = value

    for k in range(chunks):
        for copy in token_copies(k):
            copy.wait_send()
        w_copies[k].wait_send()
        row_wait(k).wait_send()
        dg_copies[k].wait()
        own_copies[k].wait()
    for copy in meta_copies:
        copy.wait_send()
    hid_copy.wait_send()
    part_copy.wait_send()
    hg_copy.wait()
    hg_store.wait()


def per_device(grad_out, routes, route_weight, hidden_saved, down_weight):
    tokens, width = grad_out.shape
    n = lax.axis_size("expert") // 2
    cap, hidden_width = hidden_saved.shape[3], hidden_saved.shape[4]
    quarter = down_weight.shape[1]
    half = 2 * quarter
    chunks = 7
    chunk = width // chunks
    rows = n * 2 * WIDE
    slots = 2 * n * cap
    hidden = hidden_saved.reshape(2 * n, cap, hidden_width).transpose(1, 0, 2)
    vmem = pl.BlockSpec(memory_space=pltpu.VMEM)
    anywhere = pl.BlockSpec(memory_space=pl.ANY)
    sem = pltpu.SemaphoreType.DMA
    flops = 2 * rows * width * (4 * tokens + half + half)
    own, other, hidden_grad, prob_grad = pl.pallas_call(
        functools.partial(kernel, n, cap, tokens, chunk, chunks, quarter),
        out_shape=(
            jax.ShapeDtypeStruct((quarter, width), F32),
            jax.ShapeDtypeStruct((quarter, width), BF16),
            jax.ShapeDtypeStruct((slots, hidden_width), BF16),
            jax.ShapeDtypeStruct((tokens, 2), F32),
        ),
        in_specs=[anywhere, vmem, vmem, anywhere, anywhere],
        out_specs=(anywhere, anywhere, anywhere, vmem),
        scratch_shapes=[
            pltpu.VMEM((chunks, 4 * tokens, chunk), BF16),
            pltpu.VMEM((4 * tokens, LANES), F32),
            pltpu.VMEM((4 * tokens, rows), BF16),
            pltpu.VMEM((4 * tokens, rows), BF16),
            pltpu.VMEM((rows, 4 * tokens), BF16),
            pltpu.VMEM((rows, chunk + LANES), BF16),
            pltpu.VMEM((rows, chunk + LANES), BF16),
            pltpu.VMEM((chunks - 1, rows, chunk), BF16),
            pltpu.VMEM((chunks - 1, rows, chunk), BF16),
            pltpu.VMEM((chunks, half, chunk), BF16),
            pltpu.VMEM((slots, hidden_width), BF16),
            pltpu.VMEM((slots, half), BF16),
            pltpu.VMEM((rows, half), BF16),
            pltpu.VMEM((half, rows), BF16),
            pltpu.VMEM((rows, half), F32),
            pltpu.VMEM((chunks, quarter, chunk), F32),
            pltpu.VMEM((chunks, quarter, chunk), BF16),
            pltpu.VMEM((slots, half), BF16),
            pltpu.VMEM((slots, half), BF16),
            pltpu.VMEM((n, LANES), F32),
            pltpu.VMEM((n, LANES), F32),
            pltpu.VMEM((n, 8, LANES), F32),
            pltpu.VMEM((2 * n, 8, LANES), F32),
            sem((2 * chunks + 1,)),
            sem((chunks, 3)),
            sem((chunks, 3)),
            sem((3,)),
            sem((3,)),
            sem,
            sem,
            sem((chunks,)),
            sem((chunks,)),
            sem((chunks,)),
            sem((chunks,)),
            sem((chunks,)),
            sem((chunks,)),
            sem((chunks + 1,)),
            sem,
            sem,
            sem,
            sem,
            sem,
            sem,
        ],
        compiler_params=pltpu.CompilerParams(
            collective_id=0, has_side_effects=True, vmem_limit_bytes=62 * 1024 * 1024
        ),
        cost_estimate=pl.CostEstimate(flops=flops, bytes_accessed=1 << 24, transcendentals=0),
    )(
        grad_out,
        routes,
        route_weight,
        hidden.reshape(slots, hidden_width),
        down_weight.reshape(quarter, width),
    )
    down_grad = own + other.astype(F32)
    hidden_grad = hidden_grad.reshape(cap, 2 * n, hidden_width).transpose(1, 0, 2)
    return (
        down_grad.reshape(1, quarter, width),
        hidden_grad.reshape(hidden_saved.shape),
        prob_grad,
    )


def solution(mesh):
    placed = (
        P(("dp", "expert"), None),
        P(("dp", "expert"), None),
        P(("dp", "expert"), None),
        P("expert", "dp", None, None, None),
        P("expert", "dp", None),
    )
    return jax.shard_map(
        per_device,
        mesh=mesh,
        in_specs=placed,
        out_specs=(
            P("expert", "dp", None),
            P("expert", "dp", None, None, None),
            P(("dp", "expert"), None),
        ),
        check_vma=False,
    )
```

```python
import functools

import jax
import jax.numpy as jnp
from jax import lax
from jax.experimental import pallas as pl
from jax.experimental.pallas import tpu as pltpu
from jax.sharding import PartitionSpec as P

MESH = pl.DeviceIdType.MESH
F32 = jnp.float32
BF16 = jnp.bfloat16
WIDE = 24
LANES = 128


def iota(shape, dim):
    return lax.broadcasted_iota(jnp.int32, shape, dim)


def kernel(
    n, cap, tokens, chunk, chunks, quarter,
    grad_ref, routes_ref, gate_ref, hidden_ref, weight_ref,
    own_ref, other_ref, hg_ref, prob_ref,
    tok, meta, place0, place1, onehot, order_back, send0, recv0, send, recv,
    wbuf, hid_all, hid_part, hid_rows, hid_t, q,
    dg_own, dg_send, hg_own, hg_send, part_out, part_in, back_out, back_in,
    load_sem, tok_ssem, tok_rsem, meta_ssem, meta_rsem, hid_ssem, hid_rsem,
    w_ssem, w_rsem, row_ssem, row_rsem, dg_ssem, dg_rsem, out_sem,
    hg_ssem, hg_rsem, part_ssem, part_rsem, back_ssem, back_rsem,
):
    d, e = lax.axis_index("dp"), lax.axis_index("expert")
    zl, i = e // n, e % n
    across = (1 - zl) * n + i
    da = 3 - d
    hq = d % 2
    db = d + 1 - 2 * hq
    hh = d // 2
    half = 2 * quarter
    span = 2 * WIDE
    rows = n * span
    slots = 2 * n * cap
    mine = pl.multiple_of(i * span, span)

    def remote(src, dst, ssem, rsem, device):
        return pltpu.make_async_remote_copy(
            src_ref=src, dst_ref=dst, send_sem=ssem, recv_sem=rsem,
            device_id=device, device_id_type=MESH,
        )

    def columns(k):
        return pl.ds(k * chunk, chunk)

    own_block = pl.multiple_of(zl * tokens, tokens)
    own_rows = pl.multiple_of(hq * quarter, quarter)
    tok_loads = [
        pltpu.make_async_copy(
            grad_ref.at[:, columns(k)], tok.at[k, pl.ds(own_block, tokens)], load_sem.at[k]
        )
        for k in range(chunks)
    ]
    w_loads = [
        pltpu.make_async_copy(
            weight_ref.at[:, columns(k)], wbuf.at[k, pl.ds(own_rows, quarter)], load_sem.at[chunks + k]
        )
        for k in range(chunks)
    ]
    hid_load = pltpu.make_async_copy(hidden_ref, hid_all, load_sem.at[2 * chunks])
    for load in tok_loads + [hid_load] + w_loads:
        load.start()

    barrier = pltpu.get_barrier_semaphore()

    def greet(j, carry):
        pl.semaphore_signal(
            barrier, inc=1, device_id=(d, (e + j) % (2 * n)), device_id_type=MESH
        )
        return carry

    lax.fori_loop(1, 2 * n, greet, 0)
    for device in ((da, e), (da, across), (db, e)):
        pl.semaphore_signal(barrier, inc=1, device_id=device, device_id_type=MESH)
    pl.semaphore_wait(barrier, 2 * n + 2)

    inner = zl == hq
    far_blocks = pl.ds(2 * tokens, 2 * tokens)

    def token_copies(k):
        here = tok.at[k, pl.ds(own_block, tokens)]
        there = tok.at[k, pl.ds(pl.multiple_of((2 + zl) * tokens, tokens), tokens)]
        both = tok.at[k, far_blocks]
        return (
            remote(here, here, tok_ssem.at[k, 0], tok_rsem.at[k, 0], (d, across)),
            remote(here, there, tok_ssem.at[k, 1], tok_rsem.at[k, 1], (da, across)),
            remote(here, there, tok_ssem.at[k, 1], tok_rsem.at[k, 2], (da, e)),
            remote(both, both, tok_ssem.at[k, 2], tok_rsem.at[k, 3], (d, across)),
        )

    def send_tokens(k):
        tok_loads[k].wait()
        beside, near, far, _ = token_copies(k)
        beside.start()
        pl.when(inner)(near.start)
        pl.when(jnp.logical_not(inner))(far.start)

    def hand_on(k):
        _, near, far, both = token_copies(k)

        @pl.when(inner)
        def _():
            near.wait_recv()
            far.wait_recv()
            both.start()

    def await_tokens(k):
        beside, _, _, both = token_copies(k)
        beside.wait_recv()
        pl.when(jnp.logical_not(inner))(both.wait_recv)

    def end_tokens(k):
        beside, near, _, both = token_copies(k)
        beside.wait_send()
        near.wait_send()
        pl.when(inner)(both.wait_send)

    send_tokens(0)

    lane = iota((tokens, LANES), 1)
    lane_f = lane.astype(F32)

    def column(array, k):
        pick = (iota((2, LANES), 0) == k).astype(F32).astype(BF16)
        return lax.dot_general(
            array, pick, (((0,), (0,)), ((), ())), preferred_element_type=F32
        )

    experts = routes_ref[...].astype(F32).astype(BF16)
    name0, name1 = column(experts, 0), column(experts, 1)
    member0 = (lane_f == name0).astype(F32)
    member1 = (lane_f == name1).astype(F32)
    before = (iota((tokens, tokens), 1) < iota((tokens, tokens), 0)).astype(F32).astype(BF16)
    earlier = jnp.dot(before, (member0 + member1).astype(BF16), preferred_element_type=F32)
    slot0 = jnp.sum(earlier * member0, axis=1, keepdims=True)
    slot1 = jnp.sum(earlier * member1, axis=1, keepdims=True)
    gates = gate_ref[...]
    info = jnp.where(lane == 0, name0, 0.0)
    info = jnp.where(lane == 1, name1, info)
    info = jnp.where(lane == 2, column(gates, 0), info)
    info = jnp.where(lane == 3, column(gates, 1), info)
    info = jnp.where(lane == 4, slot0, info)
    info = jnp.where(lane == 5, slot1, info)
    meta[pl.ds(own_block, tokens), :] = info.astype(BF16)
    meta_here = meta.at[pl.ds(own_block, tokens)]
    meta_there = meta.at[pl.ds(pl.multiple_of((2 + zl) * tokens, tokens), tokens)]
    meta_copies = [
        remote(meta_here, meta_here, meta_ssem.at[0], meta_rsem.at[0], (d, across)),
        remote(meta_here, meta_there, meta_ssem.at[1], meta_rsem.at[1], (da, e)),
        remote(meta_here, meta_there, meta_ssem.at[2], meta_rsem.at[2], (da, across)),
    ]
    for copy in meta_copies:
        copy.start()
    send_tokens(1)

    hid_load.wait()
    hid_copy = remote(
        hid_all.at[:, pl.ds(pl.multiple_of((1 - hh) * half, half), half)],
        hid_part, hid_ssem, hid_rsem, (da, e),
    )
    hid_copy.start()
    send_tokens(2)

    to = iota((slots, n * WIDE), 0)
    to = (to % n) * WIDE + (to % (2 * n)) // n * cap + to // (2 * n)
    order_back[...] = (iota((slots, n * WIDE), 1) == to).astype(F32).astype(BF16)
    hand_on(0)

    for copy in meta_copies:
        copy.wait_recv()
    plane = (zl * rows).astype(F32)
    for block in range(4):
        part = pl.ds(block * tokens, tokens)
        offset = float((block // 2) * WIDE + (block % 2) * cap)
        seen = meta[part, :].astype(F32)
        at = seen[:, 0:1] * span + seen[:, 4:5] - plane + offset
        place0[part, :] = jnp.broadcast_to(at, (tokens, LANES))
        at = seen[:, 1:2] * span + seen[:, 5:6] - plane + offset
        place1[part, :] = jnp.broadcast_to(at, (tokens, LANES))

    tile = min(LANES, rows)

    def build(t, carry):
        part = pl.ds(pl.multiple_of(t * tile, tile), tile)
        row = (iota((4 * tokens, LANES), 1) + t * tile).astype(F32)
        first = (place0[...] == row).astype(F32).astype(BF16).T
        second = (place1[...] == row).astype(F32).astype(BF16).T
        onehot[part, :] = (first + second)[:tile]
        gate0 = jnp.broadcast_to(meta[:, 2:3], (4 * tokens, LANES))
        gate1 = jnp.broadcast_to(meta[:, 3:4], (4 * tokens, LANES))
        gate = jnp.dot(first, gate0, preferred_element_type=F32)
        gate = gate + jnp.dot(second, gate1, preferred_element_type=F32)
        send0[part, pl.ds(chunk, LANES)] = gate[:tile].astype(BF16)
        return carry

    def buffers(k):
        return (send0, recv0) if k == 0 else (send.at[k - 1], recv.at[k - 1])

    pack = min(8, n)

    group_rows = pack * span
    tiles = max(1, group_rows // tile)

    def message(k, to):
        out, into = buffers(k)

        @pl.when(to != i)
        def _():
            remote(
                out.at[pl.ds(pl.multiple_of(to * span, span), span)],
                into.at[pl.ds(mine, span)],
                row_ssem.at[k], row_rsem.at[k], (d, zl * n + to),
            ).start()

    def gather(k):
        await_tokens(k)
        out, into = buffers(k)

        def step(s, carry):
            group = (i // pack + s) % (n // pack)
            if k == 0:
                lax.fori_loop(group * tiles, group * tiles + tiles, build, 0)
            part = pl.ds(pl.multiple_of(group * group_rows, group_rows), group_rows)
            out[part, pl.ds(0, chunk)] = jnp.dot(
                onehot[part, :], tok[k], preferred_element_type=F32
            ).astype(BF16)

            def issue(j, inner_carry):
                message(k, group * pack + (i + j) % pack)
                return inner_carry

            return lax.fori_loop(0, pack, issue, carry) if k == 0 else carry

        lax.fori_loop(0, n // pack, step, 0)

        def issue(j, carry):
            message(k, (i + 5 * j) % n)
            return carry

        if k > 0:
            lax.fori_loop(1, n, issue, 0)
        into[pl.ds(mine, span), :] = out[pl.ds(mine, span), :]

    def row_wait(k):
        out, into = buffers(k)
        many = pl.ds(0, (n - 1) * span)
        return remote(out.at[many], into.at[many], row_ssem.at[k], row_rsem.at[k], (db, e))

    w_copies = [
        remote(
            wbuf.at[k, pl.ds(own_rows, quarter)], wbuf.at[k, pl.ds(own_rows, quarter)],
            w_ssem.at[k], w_rsem.at[k], (db, e),
        )
        for k in range(chunks)
    ]
    dg_copies = [
        remote(dg_send.at[k], other_ref.at[:, columns(k)], dg_ssem.at[k], dg_rsem.at[k], (db, e))
        for k in range(chunks)
    ]
    own_copies = [
        pltpu.make_async_copy(dg_own.at[k], own_ref.at[:, columns(k)], out_sem.at[k])
        for k in range(chunks)
    ]

    def order_hidden():
        hid_copy.wait_recv()
        at = iota((n * WIDE, slots), 1)
        source = at % (2 * n)
        target = (source % n) * WIDE + (source // n) * cap + at // (2 * n)
        order = (iota((n * WIDE, slots), 0) == target).astype(F32).astype(BF16)
        near = hid_all[:, pl.ds(pl.multiple_of(hh * half, half), half)]
        near = jnp.dot(order, near, preferred_element_type=F32).reshape(n, 1, WIDE, half)
        far = jnp.dot(order, hid_part[...], preferred_element_type=F32).reshape(n, 1, WIDE, half)
        both = jnp.concatenate([near, far], axis=1).reshape(rows, half)
        hid_rows[...] = both.astype(BF16)

    def weigh_hidden():
        def turn(t, carry):
            part = pl.ds(pl.multiple_of(t * tile, tile), tile)
            gate = recv0[part, pl.ds(chunk, LANES)].astype(F32)[:, 0:1]
            hid_t[:, part] = (hid_rows[part, :].astype(F32) * gate).astype(BF16).T
            return carry

        lax.fori_loop(0, rows // tile, turn, 0)

    def down(k):
        if k < chunks - 1:
            row_wait(k).wait_recv()
        if k == 0:
            weigh_hidden()
        into = buffers(k)[1]
        got = into[:, pl.ds(0, chunk)]
        theirs = pl.ds(pl.multiple_of((1 - hq) * quarter, quarter), quarter)
        dg_send[k] = jnp.dot(hid_t[theirs, :], got, preferred_element_type=F32).astype(BF16)
        dg_copies[k].start()
        dg_own[k] = jnp.dot(hid_t[pl.ds(own_rows, quarter), :], got, preferred_element_type=F32)
        own_copies[k].start()

    strip = rows // 6

    def project(k):
        w_copies[k].wait_recv()
        into = buffers(k)[1]

        def step(t, carry):
            part = pl.ds(pl.multiple_of(t * strip, strip), strip)
            more = lax.dot_general(
                into[part, pl.ds(0, chunk)], wbuf[k], (((1,), (1,)), ((), ())),
                preferred_element_type=F32,
            )
            q[part, :] = more if k == 0 else q[part, :] + more
            return carry

        lax.fori_loop(0, 6, step, 0)

    for k in range(chunks):
        if k + 1 < chunks:
            hand_on(k + 1)
        gather(k)
        if k + 3 < chunks:
            send_tokens(k + 3)
        w_loads[k].wait()
        w_copies[k].start()
        if k == 0:
            order_hidden()
        if k >= 1:
            down(k - 1)
            project(k - 1)

    row_wait(chunks - 1).wait_recv()
    project(chunks - 1)
    hg_columns = pl.ds(pl.multiple_of(hh * half, half), half)
    hg_copy = remote(hg_send, hg_ref.at[:, hg_columns], hg_ssem, hg_rsem, (da, e))
    hg_store = pltpu.make_async_copy(hg_own, hg_ref.at[:, hg_columns], out_sem.at[chunks])

    def weigh(g):
        gate = recv0[:, pl.ds(chunk, LANES)].astype(F32)[:, 0:1].reshape(n, 2, WIDE, 1)[:, g]
        got = q[...].reshape(n, 2, WIDE, half)[:, g]
        got = (got * gate).reshape(n * WIDE, half).astype(BF16)
        return jnp.dot(order_back[...], got, preferred_element_type=F32).astype(BF16)

    hg_send[...] = weigh(1)
    hg_copy.start()
    sums = jnp.sum(hid_rows[...].astype(F32) * q[...], axis=1, keepdims=True)
    spread = jnp.where(
        iota((rows, LANES), 1) == iota((rows, LANES), 0) % WIDE, sums, 0.0
    ).reshape(n, 2, WIDE, LANES)
    spread = jnp.sum(spread, axis=2)
    part_out[...] = spread[:, 1]
    part_copy = remote(part_out, part_in, part_ssem, part_rsem, (da, e))
    part_copy.start()
    down(chunks - 1)
    hg_own[...] = weigh(0)
    hg_store.start()
    part_copy.wait_recv()
    total = spread[:, 0] + part_in[...]
    back_out[...] = jnp.broadcast_to(total[:, None, :], (n, 8, LANES))

    def give(j, carry):
        to = (e + j) % (2 * n)
        remote(
            back_out.at[to % n], back_in.at[e], back_ssem, back_rsem, (d, to)
        ).start()
        return carry

    lax.fori_loop(1, 2 * n, give, 0)
    back_in[e] = back_out[i]
    many = pl.ds(0, 2 * n - 1)
    remote(back_in.at[many], back_in.at[many], back_ssem, back_rsem, (db, e)).wait()
    table = back_in[...][:, 0, :]
    for k, (member, slot) in enumerate(((member0, slot0), (member1, slot1))):
        found = jnp.dot(
            member[:, : 2 * n], table, preferred_element_type=F32, precision=lax.Precision.HIGHEST
        )
        at = slot + (zl * cap).astype(F32)
        value = jnp.sum(jnp.where(lane_f == at, found, 0.0), axis=1, keepdims=True)
        prob_ref[:, k : k + 1] = value

    for k in range(chunks):
        end_tokens(k)
        w_copies[k].wait_send()
        row_wait(k).wait_send()
        dg_copies[k].wait()
        own_copies[k].wait()
    for copy in meta_copies:
        copy.wait_send()
    hid_copy.wait_send()
    part_copy.wait_send()
    hg_copy.wait()
    hg_store.wait()


def per_device(grad_out, routes, route_weight, hidden_saved, down_weight):
    tokens, width = grad_out.shape
    n = lax.axis_size("expert") // 2
    cap, hidden_width = hidden_saved.shape[3], hidden_saved.shape[4]
    quarter = down_weight.shape[1]
    half = 2 * quarter
    chunks = 7
    chunk = width // chunks
    rows = n * 2 * WIDE
    slots = 2 * n * cap
    hidden = hidden_saved.reshape(2 * n, cap, hidden_width).transpose(1, 0, 2)
    vmem = pl.BlockSpec(memory_space=pltpu.VMEM)
    anywhere = pl.BlockSpec(memory_space=pl.ANY)
    sem = pltpu.SemaphoreType.DMA
    flops = 2 * rows * width * (4 * tokens + half + half)
    own, other, hidden_grad, prob_grad = pl.pallas_call(
        functools.partial(kernel, n, cap, tokens, chunk, chunks, quarter),
        out_shape=(
            jax.ShapeDtypeStruct((quarter, width), F32),
            jax.ShapeDtypeStruct((quarter, width), BF16),
            jax.ShapeDtypeStruct((slots, hidden_width), BF16),
            jax.ShapeDtypeStruct((tokens, 2), F32),
        ),
        in_specs=[anywhere, vmem, vmem, anywhere, anywhere],
        out_specs=(anywhere, anywhere, anywhere, vmem),
        scratch_shapes=[
            pltpu.VMEM((chunks, 4 * tokens, chunk), BF16),
            pltpu.VMEM((4 * tokens, LANES), BF16),
            pltpu.VMEM((4 * tokens, LANES), F32),
            pltpu.VMEM((4 * tokens, LANES), F32),
            pltpu.VMEM((rows, 4 * tokens), BF16),
            pltpu.VMEM((slots, n * WIDE), BF16),
            pltpu.VMEM((rows, chunk + LANES), BF16),
            pltpu.VMEM((rows, chunk + LANES), BF16),
            pltpu.VMEM((chunks - 1, rows, chunk), BF16),
            pltpu.VMEM((chunks - 1, rows, chunk), BF16),
            pltpu.VMEM((chunks, half, chunk), BF16),
            pltpu.VMEM((slots, hidden_width), BF16),
            pltpu.VMEM((slots, half), BF16),
            pltpu.VMEM((rows, half), BF16),
            pltpu.VMEM((half, rows), BF16),
            pltpu.VMEM((rows, half), F32),
            pltpu.VMEM((chunks, quarter, chunk), F32),
            pltpu.VMEM((chunks, quarter, chunk), BF16),
            pltpu.VMEM((slots, half), BF16),
            pltpu.VMEM((slots, half), BF16),
            pltpu.VMEM((n, LANES), F32),
            pltpu.VMEM((n, LANES), F32),
            pltpu.VMEM((n, 8, LANES), F32),
            pltpu.VMEM((2 * n, 8, LANES), F32),
            sem((2 * chunks + 1,)),
            sem((chunks, 3)),
            sem((chunks, 4)),
            sem((3,)),
            sem((3,)),
            sem,
            sem,
            sem((chunks,)),
            sem((chunks,)),
            sem((chunks,)),
            sem((chunks,)),
            sem((chunks,)),
            sem((chunks,)),
            sem((chunks + 1,)),
            sem,
            sem,
            sem,
            sem,
            sem,
            sem,
        ],
        compiler_params=pltpu.CompilerParams(
            collective_id=0, has_side_effects=True, vmem_limit_bytes=62 * 1024 * 1024
        ),
        cost_estimate=pl.CostEstimate(flops=flops, bytes_accessed=1 << 24, transcendentals=0),
    )(
        grad_out,
        routes.T,
        route_weight.T,
        hidden.reshape(slots, hidden_width),
        down_weight.reshape(quarter, width),
    )
    down_grad = own + other.astype(F32)
    hidden_grad = hidden_grad.reshape(cap, 2 * n, hidden_width).transpose(1, 0, 2)
    return (
        down_grad.reshape(1, quarter, width),
        hidden_grad.reshape(hidden_saved.shape),
        prob_grad,
    )


def solution(mesh):
    placed = (
        P(("dp", "expert"), None),
        P(("dp", "expert"), None),
        P(("dp", "expert"), None),
        P("expert", "dp", None, None, None),
        P("expert", "dp", None),
    )
    return jax.shard_map(
        per_device,
        mesh=mesh,
        in_specs=placed,
        out_specs=(
            P("expert", "dp", None),
            P("expert", "dp", None, None, None),
            P(("dp", "expert"), None),
        ),
        check_vma=False,
    )
```

```python
import functools

import jax
import jax.numpy as jnp
from jax import lax
from jax.experimental import pallas as pl
from jax.experimental.pallas import tpu as pltpu
from jax.sharding import PartitionSpec as P

MESH = pl.DeviceIdType.MESH
F32 = jnp.float32
BF16 = jnp.bfloat16
WIDE = 24
LANES = 128


def iota(shape, dim):
    return lax.broadcasted_iota(jnp.int32, shape, dim)


def kernel(
    n, cap, tokens, chunk, chunks, quarter,
    grad_ref, routes_ref, gate_ref, hidden_ref, weight_ref,
    own_ref, other_ref, hg_ref, prob_ref,
    tok, meta, place0, place1, onehot, order_back, send0, recv0, send, recv,
    wbuf, hid_all, hid_part, hid_rows, hid_t, q,
    dg_own, dg_send, hg_own, hg_send, part_out, part_in, back_out, back_in,
    load_sem, tok_ssem, tok_rsem, meta_ssem, meta_rsem, hid_ssem, hid_rsem,
    w_ssem, w_rsem, row_ssem, row_rsem, dg_ssem, dg_rsem, out_sem,
    hg_ssem, hg_rsem, part_ssem, part_rsem, back_ssem, back_rsem,
):
    d, e = lax.axis_index("dp"), lax.axis_index("expert")
    zl, i = e // n, e % n
    across = (1 - zl) * n + i
    da = 3 - d
    hq = d % 2
    db = d + 1 - 2 * hq
    hh = d // 2
    half = 2 * quarter
    span = 2 * WIDE
    rows = n * span
    slots = 2 * n * cap
    mine = pl.multiple_of(i * span, span)

    def remote(src, dst, ssem, rsem, device):
        return pltpu.make_async_remote_copy(
            src_ref=src, dst_ref=dst, send_sem=ssem, recv_sem=rsem,
            device_id=device, device_id_type=MESH,
        )

    def columns(k):
        return pl.ds(k * chunk, chunk)

    own_block = pl.multiple_of(zl * tokens, tokens)
    own_rows = pl.multiple_of(hq * quarter, quarter)
    tok_loads = [
        pltpu.make_async_copy(
            grad_ref.at[:, columns(k)], tok.at[k, pl.ds(own_block, tokens)], load_sem.at[k]
        )
        for k in range(chunks)
    ]
    w_loads = [
        pltpu.make_async_copy(
            weight_ref.at[:, columns(k)], wbuf.at[k, pl.ds(own_rows, quarter)], load_sem.at[chunks + k]
        )
        for k in range(chunks)
    ]
    hid_load = pltpu.make_async_copy(hidden_ref, hid_all, load_sem.at[2 * chunks])
    for load in tok_loads + [hid_load] + w_loads:
        load.start()

    barrier = pltpu.get_barrier_semaphore()

    def greet(j, carry):
        pl.semaphore_signal(
            barrier, inc=1, device_id=(d, (e + j) % (2 * n)), device_id_type=MESH
        )
        return carry

    lax.fori_loop(1, 2 * n, greet, 0)
    for device in ((da, e), (da, across), (db, e)):
        pl.semaphore_signal(barrier, inc=1, device_id=device, device_id_type=MESH)
    pl.semaphore_wait(barrier, 2 * n + 2)

    inner = zl == hq
    far_blocks = pl.ds(2 * tokens, 2 * tokens)

    def token_copies(k):
        here = tok.at[k, pl.ds(own_block, tokens)]
        there = tok.at[k, pl.ds(pl.multiple_of((2 + zl) * tokens, tokens), tokens)]
        both = tok.at[k, far_blocks]
        return (
            remote(here, here, tok_ssem.at[k, 0], tok_rsem.at[k, 0], (d, across)),
            remote(here, there, tok_ssem.at[k, 1], tok_rsem.at[k, 1], (da, across)),
            remote(here, there, tok_ssem.at[k, 1], tok_rsem.at[k, 2], (da, e)),
            remote(both, both, tok_ssem.at[k, 2], tok_rsem.at[k, 3], (d, across)),
        )

    def send_tokens(k):
        tok_loads[k].wait()
        beside, near, far, _ = token_copies(k)
        beside.start()
        pl.when(inner)(near.start)
        pl.when(jnp.logical_not(inner))(far.start)

    def hand_on(k):
        _, near, far, both = token_copies(k)

        @pl.when(inner)
        def _():
            near.wait_recv()
            far.wait_recv()
            both.start()

    def await_tokens(k):
        beside, _, _, both = token_copies(k)
        beside.wait_recv()
        pl.when(jnp.logical_not(inner))(both.wait_recv)

    def end_tokens(k):
        beside, near, _, both = token_copies(k)
        beside.wait_send()
        near.wait_send()
        pl.when(inner)(both.wait_send)

    send_tokens(0)

    lane = iota((tokens, LANES), 1)
    lane_f = lane.astype(F32)

    def column(array, k):
        pick = (iota((2, LANES), 0) == k).astype(F32).astype(BF16)
        return lax.dot_general(
            array, pick, (((0,), (0,)), ((), ())), preferred_element_type=F32
        )

    experts = routes_ref[...].astype(F32).astype(BF16)
    name0, name1 = column(experts, 0), column(experts, 1)
    member0 = (lane_f == name0).astype(F32)
    member1 = (lane_f == name1).astype(F32)
    before = (iota((tokens, tokens), 1) < iota((tokens, tokens), 0)).astype(F32).astype(BF16)
    earlier = jnp.dot(before, (member0 + member1).astype(BF16), preferred_element_type=F32)
    slot0 = jnp.sum(earlier * member0, axis=1, keepdims=True)
    slot1 = jnp.sum(earlier * member1, axis=1, keepdims=True)
    gates = gate_ref[...]
    info = jnp.where(lane == 0, name0, 0.0)
    info = jnp.where(lane == 1, name1, info)
    info = jnp.where(lane == 2, column(gates, 0), info)
    info = jnp.where(lane == 3, column(gates, 1), info)
    info = jnp.where(lane == 4, slot0, info)
    info = jnp.where(lane == 5, slot1, info)
    meta[pl.ds(own_block, tokens), :] = info.astype(BF16)
    meta_here = meta.at[pl.ds(own_block, tokens)]
    meta_there = meta.at[pl.ds(pl.multiple_of((2 + zl) * tokens, tokens), tokens)]
    meta_copies = [
        remote(meta_here, meta_here, meta_ssem.at[0], meta_rsem.at[0], (d, across)),
        remote(meta_here, meta_there, meta_ssem.at[1], meta_rsem.at[1], (da, e)),
        remote(meta_here, meta_there, meta_ssem.at[2], meta_rsem.at[2], (da, across)),
    ]
    for copy in meta_copies:
        copy.start()
    send_tokens(1)

    hid_load.wait()
    hid_copy = remote(
        hid_all.at[:, pl.ds(pl.multiple_of((1 - hh) * half, half), half)],
        hid_part, hid_ssem, hid_rsem, (da, e),
    )
    hid_copy.start()
    send_tokens(2)

    hand_on(0)

    for copy in meta_copies:
        copy.wait_recv()
    plane = (zl * rows).astype(F32)
    for block in range(4):
        part = pl.ds(block * tokens, tokens)
        offset = float((block // 2) * WIDE + (block % 2) * cap)
        seen = meta[part, :].astype(F32)
        at = seen[:, 0:1] * span + seen[:, 4:5] - plane + offset
        place0[part, :] = jnp.broadcast_to(at, (tokens, LANES))
        at = seen[:, 1:2] * span + seen[:, 5:6] - plane + offset
        place1[part, :] = jnp.broadcast_to(at, (tokens, LANES))

    tile = min(LANES, rows)

    def build(t, carry):
        part = pl.ds(pl.multiple_of(t * tile, tile), tile)
        row = (iota((4 * tokens, LANES), 1) + t * tile).astype(F32)
        first = (place0[...] == row).astype(F32).astype(BF16).T
        second = (place1[...] == row).astype(F32).astype(BF16).T
        onehot[part, :] = (first + second)[:tile]
        gate0 = jnp.broadcast_to(meta[:, 2:3], (4 * tokens, LANES))
        gate1 = jnp.broadcast_to(meta[:, 3:4], (4 * tokens, LANES))
        gate = jnp.dot(first, gate0, preferred_element_type=F32)
        gate = gate + jnp.dot(second, gate1, preferred_element_type=F32)
        send0[part, pl.ds(chunk, LANES)] = gate[:tile].astype(BF16)
        return carry

    def buffers(k):
        return (send0, recv0) if k == 0 else (send.at[k - 1], recv.at[k - 1])

    pack = min(8, n)

    group_rows = pack * span
    tiles = max(1, group_rows // tile)

    def message(k, to):
        out, into = buffers(k)

        @pl.when(to != i)
        def _():
            remote(
                out.at[pl.ds(pl.multiple_of(to * span, span), span)],
                into.at[pl.ds(mine, span)],
                row_ssem.at[k], row_rsem.at[k], (d, zl * n + to),
            ).start()

    def gather(k):
        await_tokens(k)
        out, into = buffers(k)

        def step(s, carry):
            group = (i // pack + s) % (n // pack)
            if k == 0:
                lax.fori_loop(group * tiles, group * tiles + tiles, build, 0)
            part = pl.ds(pl.multiple_of(group * group_rows, group_rows), group_rows)
            out[part, pl.ds(0, chunk)] = jnp.dot(
                onehot[part, :], tok[k], preferred_element_type=F32
            ).astype(BF16)

            def issue(j, inner_carry):
                message(k, group * pack + (i + j) % pack)
                return inner_carry

            return lax.fori_loop(0, pack, issue, carry) if k == 0 else carry

        lax.fori_loop(0, n // pack, step, 0)

        def issue(j, carry):
            message(k, (i + 5 * j) % n)
            return carry

        if k > 0:
            lax.fori_loop(1, n, issue, 0)
        into[pl.ds(mine, span), :] = out[pl.ds(mine, span), :]

    def row_wait(k):
        out, into = buffers(k)
        many = pl.ds(0, (n - 1) * span)
        return remote(out.at[many], into.at[many], row_ssem.at[k], row_rsem.at[k], (db, e))

    w_copies = [
        remote(
            wbuf.at[k, pl.ds(own_rows, quarter)], wbuf.at[k, pl.ds(own_rows, quarter)],
            w_ssem.at[k], w_rsem.at[k], (db, e),
        )
        for k in range(chunks)
    ]
    dg_copies = [
        remote(dg_send.at[k], other_ref.at[:, columns(k)], dg_ssem.at[k], dg_rsem.at[k], (db, e))
        for k in range(chunks)
    ]
    own_copies = [
        pltpu.make_async_copy(dg_own.at[k], own_ref.at[:, columns(k)], out_sem.at[k])
        for k in range(chunks)
    ]

    def order_hidden():
        hid_copy.wait_recv()
        at = iota((n * WIDE, slots), 1)
        source = at % (2 * n)
        target = (source % n) * WIDE + (source // n) * cap + at // (2 * n)
        order = (iota((n * WIDE, slots), 0) == target).astype(F32).astype(BF16)
        near = hid_all[:, pl.ds(pl.multiple_of(hh * half, half), half)]
        near = jnp.dot(order, near, preferred_element_type=F32).reshape(n, 1, WIDE, half)
        far = jnp.dot(order, hid_part[...], preferred_element_type=F32).reshape(n, 1, WIDE, half)
        both = jnp.concatenate([near, far], axis=1).reshape(rows, half)
        hid_rows[...] = both.astype(BF16)

    def weigh_hidden():
        def turn(t, carry):
            part = pl.ds(pl.multiple_of(t * tile, tile), tile)
            gate = recv0[part, pl.ds(chunk, LANES)].astype(F32)[:, 0:1]
            hid_t[:, part] = (hid_rows[part, :].astype(F32) * gate).astype(BF16).T
            return carry

        lax.fori_loop(0, rows // tile, turn, 0)

    def down(k):
        row_wait(k).wait_recv()
        if k == 0:
            weigh_hidden()
        into = buffers(k)[1]
        got = into[:, pl.ds(0, chunk)]
        theirs = pl.ds(pl.multiple_of((1 - hq) * quarter, quarter), quarter)
        dg_send[k] = jnp.dot(hid_t[theirs, :], got, preferred_element_type=F32).astype(BF16)
        dg_copies[k].start()
        dg_own[k] = jnp.dot(hid_t[pl.ds(own_rows, quarter), :], got, preferred_element_type=F32)
        own_copies[k].start()

    strip = rows // 6

    def project(k):
        w_copies[k].wait_recv()
        into = buffers(k)[1]

        def step(t, carry):
            part = pl.ds(pl.multiple_of(t * strip, strip), strip)
            more = lax.dot_general(
                into[part, pl.ds(0, chunk)], wbuf[k], (((1,), (1,)), ((), ())),
                preferred_element_type=F32,
            )
            q[part, :] = more if k == 0 else q[part, :] + more
            return carry

        lax.fori_loop(0, 6, step, 0)

    def order_slots():
        to = iota((slots, n * WIDE), 0)
        to = (to % n) * WIDE + (to % (2 * n)) // n * cap + to // (2 * n)
        order_back[...] = (iota((slots, n * WIDE), 1) == to).astype(F32).astype(BF16)

    meet = 1
    lag = 3
    for k in range(chunks):
        if 1 <= k < chunks - 1:
            hand_on(k + 1)
        gather(k)
        if k == 0:
            hand_on(1)
        if k + 3 < chunks:
            send_tokens(k + 3)
        for m in ((0, 1, 2) if k == 0 else (k + 2,)):
            if m < chunks:
                w_loads[m].wait()
                w_copies[m].start()
        if k == 1:
            order_slots()
        if k == meet:
            order_hidden()
            for m in range(k):
                down(m)
        if k > meet:
            down(k - 1)
        if k > lag:
            project(k - 1 - lag)

    for k in range(chunks - 1 - lag, chunks - 1):
        project(k)
    down(chunks - 1)
    project(chunks - 1)
    hg_columns = pl.ds(pl.multiple_of(hh * half, half), half)
    hg_copy = remote(hg_send, hg_ref.at[:, hg_columns], hg_ssem, hg_rsem, (da, e))
    hg_store = pltpu.make_async_copy(hg_own, hg_ref.at[:, hg_columns], out_sem.at[chunks])

    def weigh(g):
        gate = recv0[:, pl.ds(chunk, LANES)].astype(F32)[:, 0:1].reshape(n, 2, WIDE, 1)[:, g]
        got = q[...].reshape(n, 2, WIDE, half)[:, g]
        got = (got * gate).reshape(n * WIDE, half).astype(BF16)
        return jnp.dot(order_back[...], got, preferred_element_type=F32).astype(BF16)

    sums = jnp.sum(hid_rows[...].astype(F32) * q[...], axis=1, keepdims=True)
    spread = jnp.where(
        iota((rows, LANES), 1) == iota((rows, LANES), 0) % WIDE, sums, 0.0
    ).reshape(n, 2, WIDE, LANES)
    spread = jnp.sum(spread, axis=2)
    part_out[...] = spread[:, 1]
    part_copy = remote(part_out, part_in, part_ssem, part_rsem, (da, e))
    part_copy.start()
    hg_send[...] = weigh(1)
    hg_copy.start()
    hg_own[...] = weigh(0)
    hg_store.start()
    part_copy.wait_recv()
    total = spread[:, 0] + part_in[...]
    back_out[...] = jnp.broadcast_to(total[:, None, :], (n, 8, LANES))

    def give(j, carry):
        to = (e + j) % (2 * n)
        remote(
            back_out.at[to % n], back_in.at[e], back_ssem, back_rsem, (d, to)
        ).start()
        return carry

    lax.fori_loop(1, 2 * n, give, 0)
    back_in[e] = back_out[i]
    many = pl.ds(0, 2 * n - 1)
    remote(back_in.at[many], back_in.at[many], back_ssem, back_rsem, (db, e)).wait()
    table = back_in[...][:, 0, :]
    for k, (member, slot) in enumerate(((member0, slot0), (member1, slot1))):
        found = jnp.dot(
            member[:, : 2 * n], table, preferred_element_type=F32, precision=lax.Precision.HIGHEST
        )
        at = slot + (zl * cap).astype(F32)
        value = jnp.sum(jnp.where(lane_f == at, found, 0.0), axis=1, keepdims=True)
        prob_ref[:, k : k + 1] = value

    for k in range(chunks):
        end_tokens(k)
        w_copies[k].wait_send()
        row_wait(k).wait_send()
        dg_copies[k].wait()
        own_copies[k].wait()
    for copy in meta_copies:
        copy.wait_send()
    hid_copy.wait_send()
    part_copy.wait_send()
    hg_copy.wait()
    hg_store.wait()


def per_device(grad_out, routes, route_weight, hidden_saved, down_weight):
    tokens, width = grad_out.shape
    n = lax.axis_size("expert") // 2
    cap, hidden_width = hidden_saved.shape[3], hidden_saved.shape[4]
    quarter = down_weight.shape[1]
    half = 2 * quarter
    chunks = 7
    chunk = width // chunks
    rows = n * 2 * WIDE
    slots = 2 * n * cap
    hidden = hidden_saved.reshape(2 * n, cap, hidden_width).transpose(1, 0, 2)
    vmem = pl.BlockSpec(memory_space=pltpu.VMEM)
    anywhere = pl.BlockSpec(memory_space=pl.ANY)
    sem = pltpu.SemaphoreType.DMA
    flops = 2 * rows * width * (4 * tokens + half + half)
    own, other, hidden_grad, prob_grad = pl.pallas_call(
        functools.partial(kernel, n, cap, tokens, chunk, chunks, quarter),
        out_shape=(
            jax.ShapeDtypeStruct((quarter, width), F32),
            jax.ShapeDtypeStruct((quarter, width), BF16),
            jax.ShapeDtypeStruct((slots, hidden_width), BF16),
            jax.ShapeDtypeStruct((tokens, 2), F32),
        ),
        in_specs=[anywhere, vmem, vmem, anywhere, anywhere],
        out_specs=(anywhere, anywhere, anywhere, vmem),
        scratch_shapes=[
            pltpu.VMEM((chunks, 4 * tokens, chunk), BF16),
            pltpu.VMEM((4 * tokens, LANES), BF16),
            pltpu.VMEM((4 * tokens, LANES), F32),
            pltpu.VMEM((4 * tokens, LANES), F32),
            pltpu.VMEM((rows, 4 * tokens), BF16),
            pltpu.VMEM((slots, n * WIDE), BF16),
            pltpu.VMEM((rows, chunk + LANES), BF16),
            pltpu.VMEM((rows, chunk + LANES), BF16),
            pltpu.VMEM((chunks - 1, rows, chunk), BF16),
            pltpu.VMEM((chunks - 1, rows, chunk), BF16),
            pltpu.VMEM((chunks, half, chunk), BF16),
            pltpu.VMEM((slots, hidden_width), BF16),
            pltpu.VMEM((slots, half), BF16),
            pltpu.VMEM((rows, half), BF16),
            pltpu.VMEM((half, rows), BF16),
            pltpu.VMEM((rows, half), F32),
            pltpu.VMEM((chunks, quarter, chunk), F32),
            pltpu.VMEM((chunks, quarter, chunk), BF16),
            pltpu.VMEM((slots, half), BF16),
            pltpu.VMEM((slots, half), BF16),
            pltpu.VMEM((n, LANES), F32),
            pltpu.VMEM((n, LANES), F32),
            pltpu.VMEM((n, 8, LANES), F32),
            pltpu.VMEM((2 * n, 8, LANES), F32),
            sem((2 * chunks + 1,)),
            sem((chunks, 3)),
            sem((chunks, 4)),
            sem((3,)),
            sem((3,)),
            sem,
            sem,
            sem((chunks,)),
            sem((chunks,)),
            sem((chunks,)),
            sem((chunks,)),
            sem((chunks,)),
            sem((chunks,)),
            sem((chunks + 1,)),
            sem,
            sem,
            sem,
            sem,
            sem,
            sem,
        ],
        compiler_params=pltpu.CompilerParams(
            collective_id=0, has_side_effects=True, vmem_limit_bytes=62 * 1024 * 1024
        ),
        cost_estimate=pl.CostEstimate(flops=flops, bytes_accessed=1 << 24, transcendentals=0),
    )(
        grad_out,
        routes.T,
        route_weight.T,
        hidden.reshape(slots, hidden_width),
        down_weight.reshape(quarter, width),
    )
    down_grad = own + other.astype(F32)
    hidden_grad = hidden_grad.reshape(cap, 2 * n, hidden_width).transpose(1, 0, 2)
    return (
        down_grad.reshape(1, quarter, width),
        hidden_grad.reshape(hidden_saved.shape),
        prob_grad,
    )


def solution(mesh):
    placed = (
        P(("dp", "expert"), None),
        P(("dp", "expert"), None),
        P(("dp", "expert"), None),
        P("expert", "dp", None, None, None),
        P("expert", "dp", None),
    )
    return jax.shard_map(
        per_device,
        mesh=mesh,
        in_specs=placed,
        out_specs=(
            P("expert", "dp", None),
            P("expert", "dp", None, None, None),
            P(("dp", "expert"), None),
        ),
        check_vma=False,
    )
```

```python
import functools

import jax
import jax.numpy as jnp
from jax import lax
from jax.experimental import pallas as pl
from jax.experimental.pallas import tpu as pltpu
from jax.sharding import PartitionSpec as P

MESH = pl.DeviceIdType.MESH
F32 = jnp.float32
BF16 = jnp.bfloat16
WIDE = 24
LANES = 128


def iota(shape, dim):
    return lax.broadcasted_iota(jnp.int32, shape, dim)


def kernel(
    n, cap, tokens, chunk, chunks, quarter,
    grad_ref, routes_ref, gate_ref, hidden_ref, weight_ref,
    own_ref, other_ref, hg_ref, prob_ref,
    tok, meta, place0, place1, gates0, gates1, onehot, order_back, send0, recv0, send, recv,
    wbuf, hid_all, hid_part, hid_rows, hid_t, q,
    dg_own, dg_send, hg_own, hg_send, part_out, part_in, back_out, back_in,
    load_sem, tok_ssem, tok_rsem, meta_ssem, meta_rsem, hid_ssem, hid_rsem,
    w_ssem, w_rsem, row_ssem, row_rsem, dg_ssem, dg_rsem, out_sem,
    hg_ssem, hg_rsem, part_ssem, part_rsem, back_ssem, back_rsem,
):
    d, e = lax.axis_index("dp"), lax.axis_index("expert")
    zl, i = e // n, e % n
    across = (1 - zl) * n + i
    da = 3 - d
    hq = d % 2
    db = d + 1 - 2 * hq
    hh = d // 2
    half = 2 * quarter
    span = 2 * WIDE
    rows = n * span
    slots = 2 * n * cap
    mine = pl.multiple_of(i * span, span)

    def remote(src, dst, ssem, rsem, device):
        return pltpu.make_async_remote_copy(
            src_ref=src, dst_ref=dst, send_sem=ssem, recv_sem=rsem,
            device_id=device, device_id_type=MESH,
        )

    def columns(k):
        return pl.ds(k * chunk, chunk)

    own_block = pl.multiple_of(zl * tokens, tokens)
    own_rows = pl.multiple_of(hq * quarter, quarter)
    tok_loads = [
        pltpu.make_async_copy(
            grad_ref.at[:, columns(k)], tok.at[k, pl.ds(own_block, tokens)], load_sem.at[k]
        )
        for k in range(chunks)
    ]
    w_loads = [
        pltpu.make_async_copy(
            weight_ref.at[:, columns(k)], wbuf.at[k, pl.ds(own_rows, quarter)], load_sem.at[chunks + k]
        )
        for k in range(chunks)
    ]
    hid_load = pltpu.make_async_copy(hidden_ref, hid_all, load_sem.at[2 * chunks])
    for load in tok_loads + [hid_load] + w_loads:
        load.start()

    barrier = pltpu.get_barrier_semaphore()

    def greet(j, carry):
        pl.semaphore_signal(
            barrier, inc=1, device_id=(d, (e + j) % (2 * n)), device_id_type=MESH
        )
        return carry

    lax.fori_loop(1, 2 * n, greet, 0)
    for device in ((da, e), (da, across), (db, e)):
        pl.semaphore_signal(barrier, inc=1, device_id=device, device_id_type=MESH)
    pl.semaphore_wait(barrier, 2 * n + 2)

    inner = zl == hq
    far_blocks = pl.ds(2 * tokens, 2 * tokens)

    def token_copies(k):
        here = tok.at[k, pl.ds(own_block, tokens)]
        there = tok.at[k, pl.ds(pl.multiple_of((2 + zl) * tokens, tokens), tokens)]
        both = tok.at[k, far_blocks]
        return (
            remote(here, here, tok_ssem.at[k, 0], tok_rsem.at[k, 0], (d, across)),
            remote(here, there, tok_ssem.at[k, 1], tok_rsem.at[k, 1], (da, across)),
            remote(here, there, tok_ssem.at[k, 1], tok_rsem.at[k, 2], (da, e)),
            remote(both, both, tok_ssem.at[k, 2], tok_rsem.at[k, 3], (d, across)),
        )

    def send_tokens(k):
        tok_loads[k].wait()
        beside, near, far, _ = token_copies(k)
        beside.start()
        pl.when(inner)(near.start)
        pl.when(jnp.logical_not(inner))(far.start)

    def hand_on(k):
        _, near, far, both = token_copies(k)

        @pl.when(inner)
        def _():
            near.wait_recv()
            far.wait_recv()
            both.start()

    def await_tokens(k):
        beside, _, _, both = token_copies(k)
        beside.wait_recv()
        pl.when(jnp.logical_not(inner))(both.wait_recv)

    def end_tokens(k):
        beside, near, _, both = token_copies(k)
        beside.wait_send()
        near.wait_send()
        pl.when(inner)(both.wait_send)

    meta[zl] = jnp.zeros((16, 256), BF16)
    meta[zl, 0:2, 0:tokens] = routes_ref[...].astype(F32).astype(BF16)
    meta[zl, 2:4, 0:tokens] = gate_ref[...]
    meta_copies = [
        remote(meta.at[zl], meta.at[zl], meta_ssem.at[0], meta_rsem.at[0], (d, across)),
        remote(meta.at[zl], meta.at[2 + zl], meta_ssem.at[1], meta_rsem.at[1], (da, e)),
        remote(meta.at[zl], meta.at[2 + zl], meta_ssem.at[2], meta_rsem.at[2], (da, across)),
    ]
    for copy in meta_copies:
        copy.start()
    send_tokens(0)

    send_tokens(1)

    hid_load.wait()
    hid_copy = remote(
        hid_all.at[:, pl.ds(pl.multiple_of((1 - hh) * half, half), half)],
        hid_part, hid_ssem, hid_rsem, (da, e),
    )
    hid_copy.start()
    send_tokens(2)

    hand_on(0)

    for copy in meta_copies:
        copy.wait_recv()
    lane_f = iota((tokens, LANES), 1).astype(F32)
    before = (iota((tokens, tokens), 1) < iota((tokens, tokens), 0)).astype(F32).astype(BF16)

    def column(block, k):
        pick = (iota((2, LANES), 0) == k % 2).astype(F32).astype(BF16)
        row = meta[block, k // 2 * 2 : k // 2 * 2 + 2, 0:tokens]
        return lax.dot_general(
            row, pick, (((0,), (0,)), ((), ())), preferred_element_type=F32
        )

    def slots_of(block):
        names = column(block, 0), column(block, 1)
        members = [(lane_f == name).astype(F32) for name in names]
        earlier = jnp.dot(
            before, (members[0] + members[1]).astype(BF16), preferred_element_type=F32
        )
        places = [jnp.sum(earlier * member, axis=1, keepdims=True) for member in members]
        return names, members, places

    plane = (zl * rows).astype(F32)
    for block in range(4):
        part = pl.ds(block * tokens, tokens)
        offset = float((block // 2) * WIDE + (block % 2) * cap)
        names, _, places = slots_of(block)
        place0[part, :] = names[0] * span + (places[0] - plane + offset)
        place1[part, :] = names[1] * span + (places[1] - plane + offset)
        gates0[part, :] = column(block, 2).astype(BF16)
        gates1[part, :] = column(block, 3).astype(BF16)

    tile = min(LANES, rows)

    def build(t, carry):
        part = pl.ds(pl.multiple_of(t * tile, tile), tile)
        row = (iota((4 * tokens, LANES), 1) + t * tile).astype(F32)
        first = (place0[...] == row).astype(F32).astype(BF16).T
        second = (place1[...] == row).astype(F32).astype(BF16).T
        onehot[part, :] = (first + second)[:tile]
        gate = jnp.dot(first, gates0[...], preferred_element_type=F32)
        gate = gate + jnp.dot(second, gates1[...], preferred_element_type=F32)
        send0[part, pl.ds(chunk, LANES)] = gate[:tile].astype(BF16)
        return carry

    def buffers(k):
        return (send0, recv0) if k == 0 else (send.at[k - 1], recv.at[k - 1])

    pack = min(8, n)

    group_rows = pack * span
    tiles = max(1, group_rows // tile)

    def message(k, to):
        out, into = buffers(k)

        @pl.when(to != i)
        def _():
            remote(
                out.at[pl.ds(pl.multiple_of(to * span, span), span)],
                into.at[pl.ds(mine, span)],
                row_ssem.at[k], row_rsem.at[k], (d, zl * n + to),
            ).start()

    def gather(k):
        await_tokens(k)
        out, into = buffers(k)

        def step(s, carry):
            group = (i // pack + s) % (n // pack)
            if k == 0:
                lax.fori_loop(group * tiles, group * tiles + tiles, build, 0)
            part = pl.ds(pl.multiple_of(group * group_rows, group_rows), group_rows)
            out[part, pl.ds(0, chunk)] = jnp.dot(
                onehot[part, :], tok[k], preferred_element_type=F32
            ).astype(BF16)

            def issue(j, inner_carry):
                message(k, group * pack + (i + j) % pack)
                return inner_carry

            return lax.fori_loop(0, pack, issue, carry) if k == 0 else carry

        lax.fori_loop(0, n // pack, step, 0)

        def issue(j, carry):
            message(k, (i + 5 * j) % n)
            return carry

        if k > 0:
            lax.fori_loop(1, n, issue, 0)
        into[pl.ds(mine, span), :] = out[pl.ds(mine, span), :]

    def row_wait(k):
        out, into = buffers(k)
        many = pl.ds(0, (n - 1) * span)
        return remote(out.at[many], into.at[many], row_ssem.at[k], row_rsem.at[k], (db, e))

    w_copies = [
        remote(
            wbuf.at[k, pl.ds(own_rows, quarter)], wbuf.at[k, pl.ds(own_rows, quarter)],
            w_ssem.at[k], w_rsem.at[k], (db, e),
        )
        for k in range(chunks)
    ]
    dg_copies = [
        remote(dg_send.at[k], other_ref.at[:, columns(k)], dg_ssem.at[k], dg_rsem.at[k], (db, e))
        for k in range(chunks)
    ]
    own_copies = [
        pltpu.make_async_copy(dg_own.at[k], own_ref.at[:, columns(k)], out_sem.at[k])
        for k in range(chunks)
    ]

    def order_hidden():
        hid_copy.wait_recv()
        at = iota((n * WIDE, slots), 1)
        source = at % (2 * n)
        target = (source % n) * WIDE + (source // n) * cap + at // (2 * n)
        order = (iota((n * WIDE, slots), 0) == target).astype(F32).astype(BF16)
        near = hid_all[:, pl.ds(pl.multiple_of(hh * half, half), half)]
        near = jnp.dot(order, near, preferred_element_type=F32).reshape(n, 1, WIDE, half)
        far = jnp.dot(order, hid_part[...], preferred_element_type=F32).reshape(n, 1, WIDE, half)
        both = jnp.concatenate([near, far], axis=1).reshape(rows, half)
        hid_rows[...] = both.astype(BF16)

    def weigh_hidden():
        def turn(t, carry):
            part = pl.ds(pl.multiple_of(t * tile, tile), tile)
            gate = recv0[part, pl.ds(chunk, LANES)].astype(F32)[:, 0:1]
            hid_t[:, part] = (hid_rows[part, :].astype(F32) * gate).astype(BF16).T
            return carry

        lax.fori_loop(0, rows // tile, turn, 0)

    def down(k):
        row_wait(k).wait_recv()
        if k == 0:
            weigh_hidden()
        into = buffers(k)[1]
        got = into[:, pl.ds(0, chunk)]
        theirs = pl.ds(pl.multiple_of((1 - hq) * quarter, quarter), quarter)
        dg_send[k] = jnp.dot(hid_t[theirs, :], got, preferred_element_type=F32).astype(BF16)
        dg_copies[k].start()
        dg_own[k] = jnp.dot(hid_t[pl.ds(own_rows, quarter), :], got, preferred_element_type=F32)
        own_copies[k].start()

    strip = rows // 6

    def project(k):
        w_copies[k].wait_recv()
        into = buffers(k)[1]

        def step(t, carry):
            part = pl.ds(pl.multiple_of(t * strip, strip), strip)
            more = lax.dot_general(
                into[part, pl.ds(0, chunk)], wbuf[k], (((1,), (1,)), ((), ())),
                preferred_element_type=F32,
            )
            q[part, :] = more if k == 0 else q[part, :] + more
            return carry

        lax.fori_loop(0, 6, step, 0)

    def order_slots():
        to = iota((slots, n * WIDE), 0)
        to = (to % n) * WIDE + (to % (2 * n)) // n * cap + to // (2 * n)
        order_back[...] = (iota((slots, n * WIDE), 1) == to).astype(F32).astype(BF16)

    meet = 1
    lag = 3
    for k in range(chunks):
        if 1 <= k < chunks - 1:
            hand_on(k + 1)
        gather(k)
        if k == 0:
            hand_on(1)
        if k + 3 < chunks:
            send_tokens(k + 3)
        for m in ((0, 1, 2) if k == 0 else (k + 2,)):
            if m < chunks:
                w_loads[m].wait()
                w_copies[m].start()
        if k == 1:
            order_slots()
        if k == meet:
            order_hidden()
            for m in range(k):
                down(m)
        if k > meet:
            down(k - 1)
        if k > lag:
            project(k - 1 - lag)

    for k in range(chunks - 1 - lag, chunks - 1):
        project(k)
    down(chunks - 1)
    project(chunks - 1)
    hg_columns = pl.ds(pl.multiple_of(hh * half, half), half)
    hg_copy = remote(hg_send, hg_ref.at[:, hg_columns], hg_ssem, hg_rsem, (da, e))
    hg_store = pltpu.make_async_copy(hg_own, hg_ref.at[:, hg_columns], out_sem.at[chunks])

    def weigh(g):
        gate = recv0[:, pl.ds(chunk, LANES)].astype(F32)[:, 0:1].reshape(n, 2, WIDE, 1)[:, g]
        got = q[...].reshape(n, 2, WIDE, half)[:, g]
        got = (got * gate).reshape(n * WIDE, half).astype(BF16)
        return jnp.dot(order_back[...], got, preferred_element_type=F32).astype(BF16)

    sums = jnp.sum(hid_rows[...].astype(F32) * q[...], axis=1, keepdims=True)
    spread = jnp.where(
        iota((rows, LANES), 1) == iota((rows, LANES), 0) % WIDE, sums, 0.0
    ).reshape(n, 2, WIDE, LANES)
    spread = jnp.sum(spread, axis=2)
    part_out[...] = spread[:, 1]
    part_copy = remote(part_out, part_in, part_ssem, part_rsem, (da, e))
    part_copy.start()
    hg_send[...] = weigh(1)
    hg_copy.start()
    hg_own[...] = weigh(0)
    hg_store.start()
    part_copy.wait_recv()
    total = spread[:, 0] + part_in[...]
    back_out[...] = jnp.broadcast_to(total[:, None, :], (n, 8, LANES))

    def give(j, carry):
        to = (e + j) % (2 * n)
        remote(
            back_out.at[to % n], back_in.at[e], back_ssem, back_rsem, (d, to)
        ).start()
        return carry

    lax.fori_loop(1, 2 * n, give, 0)
    back_in[e] = back_out[i]
    many = pl.ds(0, 2 * n - 1)
    remote(back_in.at[many], back_in.at[many], back_ssem, back_rsem, (db, e)).wait()
    table = back_in[...][:, 0, :]
    own_rows_in = pl.ds(own_block, tokens)
    base = plane - (zl * cap).astype(F32)
    for k, place in enumerate((place0, place1)):
        at = place[own_rows_in, :] + base
        name = jnp.floor((at + 0.5) / span)
        member = (lane_f == name).astype(F32)
        slot = (at - name * span)[:, 0:1]
        found = jnp.dot(
            member[:, : 2 * n], table, preferred_element_type=F32, precision=lax.Precision.HIGHEST
        )
        at = slot + (zl * cap).astype(F32)
        value = jnp.sum(jnp.where(lane_f == at, found, 0.0), axis=1, keepdims=True)
        prob_ref[:, k : k + 1] = value

    for k in range(chunks):
        end_tokens(k)
        w_copies[k].wait_send()
        row_wait(k).wait_send()
        dg_copies[k].wait()
        own_copies[k].wait()
    for copy in meta_copies:
        copy.wait_send()
    hid_copy.wait_send()
    part_copy.wait_send()
    hg_copy.wait()
    hg_store.wait()


def per_device(grad_out, routes, route_weight, hidden_saved, down_weight):
    tokens, width = grad_out.shape
    n = lax.axis_size("expert") // 2
    cap, hidden_width = hidden_saved.shape[3], hidden_saved.shape[4]
    quarter = down_weight.shape[1]
    half = 2 * quarter
    chunks = 7
    chunk = width // chunks
    rows = n * 2 * WIDE
    slots = 2 * n * cap
    hidden = hidden_saved.reshape(2 * n, cap, hidden_width).transpose(1, 0, 2)
    vmem = pl.BlockSpec(memory_space=pltpu.VMEM)
    anywhere = pl.BlockSpec(memory_space=pl.ANY)
    sem = pltpu.SemaphoreType.DMA
    flops = 2 * rows * width * (4 * tokens + half + half)
    own, other, hidden_grad, prob_grad = pl.pallas_call(
        functools.partial(kernel, n, cap, tokens, chunk, chunks, quarter),
        out_shape=(
            jax.ShapeDtypeStruct((quarter, width), F32),
            jax.ShapeDtypeStruct((quarter, width), BF16),
            jax.ShapeDtypeStruct((slots, hidden_width), BF16),
            jax.ShapeDtypeStruct((tokens, 2), F32),
        ),
        in_specs=[anywhere, vmem, vmem, anywhere, anywhere],
        out_specs=(anywhere, anywhere, anywhere, vmem),
        scratch_shapes=[
            pltpu.VMEM((chunks, 4 * tokens, chunk), BF16),
            pltpu.VMEM((4, 16, 256), BF16),
            pltpu.VMEM((4 * tokens, LANES), F32),
            pltpu.VMEM((4 * tokens, LANES), F32),
            pltpu.VMEM((4 * tokens, LANES), BF16),
            pltpu.VMEM((4 * tokens, LANES), BF16),
            pltpu.VMEM((rows, 4 * tokens), BF16),
            pltpu.VMEM((slots, n * WIDE), BF16),
            pltpu.VMEM((rows, chunk + LANES), BF16),
            pltpu.VMEM((rows, chunk + LANES), BF16),
            pltpu.VMEM((chunks - 1, rows, chunk), BF16),
            pltpu.VMEM((chunks - 1, rows, chunk), BF16),
            pltpu.VMEM((chunks, half, chunk), BF16),
            pltpu.VMEM((slots, hidden_width), BF16),
            pltpu.VMEM((slots, half), BF16),
            pltpu.VMEM((rows, half), BF16),
            pltpu.VMEM((half, rows), BF16),
            pltpu.VMEM((rows, half), F32),
            pltpu.VMEM((chunks, quarter, chunk), F32),
            pltpu.VMEM((chunks, quarter, chunk), BF16),
            pltpu.VMEM((slots, half), BF16),
            pltpu.VMEM((slots, half), BF16),
            pltpu.VMEM((n, LANES), F32),
            pltpu.VMEM((n, LANES), F32),
            pltpu.VMEM((n, 8, LANES), F32),
            pltpu.VMEM((2 * n, 8, LANES), F32),
            sem((2 * chunks + 1,)),
            sem((chunks, 3)),
            sem((chunks, 4)),
            sem((3,)),
            sem((3,)),
            sem,
            sem,
            sem((chunks,)),
            sem((chunks,)),
            sem((chunks,)),
            sem((chunks,)),
            sem((chunks,)),
            sem((chunks,)),
            sem((chunks + 1,)),
            sem,
            sem,
            sem,
            sem,
            sem,
            sem,
        ],
        compiler_params=pltpu.CompilerParams(
            collective_id=0, has_side_effects=True, vmem_limit_bytes=62 * 1024 * 1024
        ),
        cost_estimate=pl.CostEstimate(flops=flops, bytes_accessed=1 << 24, transcendentals=0),
    )(
        grad_out,
        routes.T,
        route_weight.T,
        hidden.reshape(slots, hidden_width),
        down_weight.reshape(quarter, width),
    )
    down_grad = own + other.astype(F32)
    hidden_grad = hidden_grad.reshape(cap, 2 * n, hidden_width).transpose(1, 0, 2)
    return (
        down_grad.reshape(1, quarter, width),
        hidden_grad.reshape(hidden_saved.shape),
        prob_grad,
    )


def solution(mesh):
    placed = (
        P(("dp", "expert"), None),
        P(("dp", "expert"), None),
        P(("dp", "expert"), None),
        P("expert", "dp", None, None, None),
        P("expert", "dp", None),
    )
    return jax.shard_map(
        per_device,
        mesh=mesh,
        in_specs=placed,
        out_specs=(
            P("expert", "dp", None),
            P("expert", "dp", None, None, None),
            P(("dp", "expert"), None),
        ),
        check_vma=False,
    )
```

```python
import functools

import jax
import jax.numpy as jnp
from jax import lax
from jax.experimental import pallas as pl
from jax.experimental.pallas import tpu as pltpu
from jax.sharding import PartitionSpec as P

MESH = pl.DeviceIdType.MESH
F32 = jnp.float32
BF16 = jnp.bfloat16
WIDE = 24
LANES = 128


def iota(shape, dim):
    return lax.broadcasted_iota(jnp.int32, shape, dim)


def kernel(
    n, cap, tokens, chunk, chunks, quarter,
    grad_ref, routes_ref, gate_ref, hidden_ref, weight_ref,
    own_ref, other_ref, hg_ref, prob_ref,
    tok, meta, place0, place1, gates0, gates1, onehot, order_back, send0, recv0, send, recv,
    wbuf, hid_all, hid_part, hid_rows, hid_t, q,
    dg_own, dg_send, hg_own, hg_send, part_out, part_in, back_out, back_in,
    load_sem, tok_ssem, tok_rsem, meta_ssem, meta_rsem, hid_ssem, hid_rsem,
    w_ssem, w_rsem, row_ssem, row_rsem, dg_ssem, dg_rsem, out_sem,
    hg_ssem, hg_rsem, part_ssem, part_rsem, back_ssem, back_rsem,
):
    d, e = lax.axis_index("dp"), lax.axis_index("expert")
    zl, i = e // n, e % n
    across = (1 - zl) * n + i
    da = 3 - d
    hq = d % 2
    db = d + 1 - 2 * hq
    hh = d // 2
    half = 2 * quarter
    span = 2 * WIDE
    rows = n * span
    slots = 2 * n * cap
    mine = pl.multiple_of(i * span, span)

    def remote(src, dst, ssem, rsem, device):
        return pltpu.make_async_remote_copy(
            src_ref=src, dst_ref=dst, send_sem=ssem, recv_sem=rsem,
            device_id=device, device_id_type=MESH,
        )

    def columns(k):
        return pl.ds(k * chunk, chunk)

    own_block = pl.multiple_of(zl * tokens, tokens)
    own_rows = pl.multiple_of(hq * quarter, quarter)
    tok_loads = [
        pltpu.make_async_copy(
            grad_ref.at[:, columns(k)], tok.at[k, pl.ds(own_block, tokens)], load_sem.at[k]
        )
        for k in range(chunks)
    ]
    w_loads = [
        pltpu.make_async_copy(
            weight_ref.at[:, columns(k)], wbuf.at[k, pl.ds(own_rows, quarter)], load_sem.at[chunks + k]
        )
        for k in range(chunks)
    ]
    hid_load = pltpu.make_async_copy(hidden_ref, hid_all, load_sem.at[2 * chunks])
    for load in tok_loads + [hid_load] + w_loads:
        load.start()

    barrier = pltpu.get_barrier_semaphore()

    def greet(j, carry):
        pl.semaphore_signal(
            barrier, inc=1, device_id=(d, (e + j) % (2 * n)), device_id_type=MESH
        )
        return carry

    lax.fori_loop(1, 2 * n, greet, 0)
    for device in ((da, e), (da, across), (db, e)):
        pl.semaphore_signal(barrier, inc=1, device_id=device, device_id_type=MESH)
    pl.semaphore_wait(barrier, 2 * n + 2)

    inner = zl == hq
    far_blocks = pl.ds(2 * tokens, 2 * tokens)

    def token_copies(k):
        here = tok.at[k, pl.ds(own_block, tokens)]
        there = tok.at[k, pl.ds(pl.multiple_of((2 + zl) * tokens, tokens), tokens)]
        both = tok.at[k, far_blocks]
        return (
            remote(here, here, tok_ssem.at[k, 0], tok_rsem.at[k, 0], (d, across)),
            remote(here, there, tok_ssem.at[k, 1], tok_rsem.at[k, 1], (da, across)),
            remote(here, there, tok_ssem.at[k, 1], tok_rsem.at[k, 2], (da, e)),
            remote(both, both, tok_ssem.at[k, 2], tok_rsem.at[k, 3], (d, across)),
        )

    def send_tokens(k):
        tok_loads[k].wait()
        beside, near, far, _ = token_copies(k)
        beside.start()
        pl.when(inner)(near.start)
        pl.when(jnp.logical_not(inner))(far.start)

    def hand_on(k):
        _, near, far, both = token_copies(k)

        @pl.when(inner)
        def _():
            near.wait_recv()
            far.wait_recv()
            both.start()

    def await_tokens(k):
        beside, _, _, both = token_copies(k)
        beside.wait_recv()
        pl.when(jnp.logical_not(inner))(both.wait_recv)

    def end_tokens(k):
        beside, near, _, both = token_copies(k)
        beside.wait_send()
        near.wait_send()
        pl.when(inner)(both.wait_send)

    meta[zl] = jnp.zeros((16, 256), BF16)
    meta[zl, 0:2, 0:tokens] = routes_ref[...].astype(F32).astype(BF16)
    meta[zl, 2:4, 0:tokens] = gate_ref[...]
    meta_copies = [
        remote(meta.at[zl], meta.at[zl], meta_ssem.at[0], meta_rsem.at[0], (d, across)),
        remote(meta.at[zl], meta.at[2 + zl], meta_ssem.at[1], meta_rsem.at[1], (da, e)),
        remote(meta.at[zl], meta.at[2 + zl], meta_ssem.at[2], meta_rsem.at[2], (da, across)),
    ]
    for copy in meta_copies:
        copy.start()
    send_tokens(0)

    send_tokens(1)

    hid_load.wait()
    hid_copy = remote(
        hid_all.at[:, pl.ds(pl.multiple_of((1 - hh) * half, half), half)],
        hid_part, hid_ssem, hid_rsem, (da, e),
    )
    send_tokens(2)
    hid_copy.start()

    hand_on(0)

    for copy in meta_copies:
        copy.wait_recv()
    lane_f = iota((tokens, LANES), 1).astype(F32)
    before = (iota((tokens, tokens), 1) < iota((tokens, tokens), 0)).astype(F32).astype(BF16)

    def column(block, k):
        pick = (iota((2, LANES), 0) == k % 2).astype(F32).astype(BF16)
        row = meta[block, k // 2 * 2 : k // 2 * 2 + 2, 0:tokens]
        return lax.dot_general(
            row, pick, (((0,), (0,)), ((), ())), preferred_element_type=F32
        )

    def slots_of(block):
        names = column(block, 0), column(block, 1)
        members = [(lane_f == name).astype(F32) for name in names]
        earlier = jnp.dot(
            before, (members[0] + members[1]).astype(BF16), preferred_element_type=F32
        )
        places = [jnp.sum(earlier * member, axis=1, keepdims=True) for member in members]
        return names, members, places

    plane = (zl * rows).astype(F32)
    for block in range(4):
        part = pl.ds(block * tokens, tokens)
        offset = float((block // 2) * WIDE + (block % 2) * cap)
        names, _, places = slots_of(block)
        place0[part, :] = names[0] * span + (places[0] - plane + offset)
        place1[part, :] = names[1] * span + (places[1] - plane + offset)
        gates0[part, :] = column(block, 2).astype(BF16)
        gates1[part, :] = column(block, 3).astype(BF16)

    tile = min(LANES, rows)

    def build(t, carry):
        part = pl.ds(pl.multiple_of(t * tile, tile), tile)
        row = (iota((4 * tokens, LANES), 1) + t * tile).astype(F32)
        first = (place0[...] == row).astype(F32).astype(BF16).T
        second = (place1[...] == row).astype(F32).astype(BF16).T
        onehot[part, :] = (first + second)[:tile]
        gate = jnp.dot(first, gates0[...], preferred_element_type=F32)
        gate = gate + jnp.dot(second, gates1[...], preferred_element_type=F32)
        send0[part, pl.ds(chunk, LANES)] = gate[:tile].astype(BF16)
        return carry

    def buffers(k):
        return (send0, recv0) if k == 0 else (send.at[k - 1], recv.at[k - 1])

    pack = min(8, n)

    group_rows = pack * span
    tiles = max(1, group_rows // tile)

    def message(k, to):
        out, into = buffers(k)

        @pl.when(to != i)
        def _():
            remote(
                out.at[pl.ds(pl.multiple_of(to * span, span), span)],
                into.at[pl.ds(mine, span)],
                row_ssem.at[k], row_rsem.at[k], (d, zl * n + to),
            ).start()

    def gather(k):
        await_tokens(k)
        out, into = buffers(k)

        def step(s, carry):
            group = (i // pack + s) % (n // pack)
            if k == 0:
                lax.fori_loop(group * tiles, group * tiles + tiles, build, 0)
            part = pl.ds(pl.multiple_of(group * group_rows, group_rows), group_rows)
            out[part, pl.ds(0, chunk)] = jnp.dot(
                onehot[part, :], tok[k], preferred_element_type=F32
            ).astype(BF16)

            def issue(j, inner_carry):
                message(k, group * pack + (i + j) % pack)
                return inner_carry

            return lax.fori_loop(0, pack, issue, carry) if k == 0 else carry

        lax.fori_loop(0, n // pack, step, 0)

        def issue(j, carry):
            message(k, (i + 5 * j) % n)
            return carry

        if k > 0:
            lax.fori_loop(1, n, issue, 0)
        into[pl.ds(mine, span), :] = out[pl.ds(mine, span), :]

    def row_wait(k):
        out, into = buffers(k)
        many = pl.ds(0, (n - 1) * span)
        return remote(out.at[many], into.at[many], row_ssem.at[k], row_rsem.at[k], (db, e))

    w_copies = [
        remote(
            wbuf.at[k, pl.ds(own_rows, quarter)], wbuf.at[k, pl.ds(own_rows, quarter)],
            w_ssem.at[k], w_rsem.at[k], (db, e),
        )
        for k in range(chunks)
    ]
    dg_copies = [
        remote(dg_send.at[k], other_ref.at[:, columns(k)], dg_ssem.at[k], dg_rsem.at[k], (db, e))
        for k in range(chunks)
    ]
    own_copies = [
        pltpu.make_async_copy(dg_own.at[k], own_ref.at[:, columns(k)], out_sem.at[k])
        for k in range(chunks)
    ]

    def order_hidden():
        hid_copy.wait_recv()
        at = iota((n * WIDE, slots), 1)
        source = at % (2 * n)
        target = (source % n) * WIDE + (source // n) * cap + at // (2 * n)
        order = (iota((n * WIDE, slots), 0) == target).astype(F32).astype(BF16)
        near = hid_all[:, pl.ds(pl.multiple_of(hh * half, half), half)]
        near = jnp.dot(order, near, preferred_element_type=F32).reshape(n, 1, WIDE, half)
        far = jnp.dot(order, hid_part[...], preferred_element_type=F32).reshape(n, 1, WIDE, half)
        both = jnp.concatenate([near, far], axis=1).reshape(rows, half)
        hid_rows[...] = both.astype(BF16)

    def weigh_hidden():
        def turn(t, carry):
            part = pl.ds(pl.multiple_of(t * tile, tile), tile)
            gate = recv0[part, pl.ds(chunk, LANES)].astype(F32)[:, 0:1]
            hid_t[:, part] = (hid_rows[part, :].astype(F32) * gate).astype(BF16).T
            return carry

        lax.fori_loop(0, rows // tile, turn, 0)

    def down(k):
        row_wait(k).wait_recv()
        if k == 0:
            weigh_hidden()
        into = buffers(k)[1]
        got = into[:, pl.ds(0, chunk)]
        theirs = pl.ds(pl.multiple_of((1 - hq) * quarter, quarter), quarter)
        dg_send[k] = jnp.dot(hid_t[theirs, :], got, preferred_element_type=F32).astype(BF16)
        dg_copies[k].start()
        dg_own[k] = jnp.dot(hid_t[pl.ds(own_rows, quarter), :], got, preferred_element_type=F32)
        own_copies[k].start()

    strip = rows // 6

    def project(k):
        w_copies[k].wait_recv()
        into = buffers(k)[1]

        def step(t, carry):
            part = pl.ds(pl.multiple_of(t * strip, strip), strip)
            more = lax.dot_general(
                into[part, pl.ds(0, chunk)], wbuf[k], (((1,), (1,)), ((), ())),
                preferred_element_type=F32,
            )
            q[part, :] = more if k == 0 else q[part, :] + more
            return carry

        lax.fori_loop(0, 6, step, 0)

    def order_slots():
        to = iota((slots, n * WIDE), 0)
        to = (to % n) * WIDE + (to % (2 * n)) // n * cap + to // (2 * n)
        order_back[...] = (iota((slots, n * WIDE), 1) == to).astype(F32).astype(BF16)

    meet = 1
    lag = 3
    for k in range(chunks):
        if 1 <= k < chunks - 1:
            hand_on(k + 1)
        gather(k)
        if k == 0:
            hand_on(1)
        if k + 3 < chunks:
            send_tokens(k + 3)
        for m in ((0, 1, 2) if k == 0 else (k + 2,)):
            if m < chunks:
                w_loads[m].wait()
                w_copies[m].start()
        if k == 1:
            order_slots()
        if k == meet:
            order_hidden()
            for m in range(k):
                down(m)
        if k > meet:
            down(k - 1)
        if k > lag:
            project(k - 1 - lag)

    for k in range(chunks - 1 - lag, chunks - 1):
        project(k)
    down(chunks - 1)
    project(chunks - 1)
    hg_columns = pl.ds(pl.multiple_of(hh * half, half), half)
    hg_copy = remote(hg_send, hg_ref.at[:, hg_columns], hg_ssem, hg_rsem, (da, e))
    hg_store = pltpu.make_async_copy(hg_own, hg_ref.at[:, hg_columns], out_sem.at[chunks])

    def weigh(g):
        gate = recv0[:, pl.ds(chunk, LANES)].astype(F32)[:, 0:1].reshape(n, 2, WIDE, 1)[:, g]
        got = q[...].reshape(n, 2, WIDE, half)[:, g]
        got = (got * gate).reshape(n * WIDE, half).astype(BF16)
        return jnp.dot(order_back[...], got, preferred_element_type=F32).astype(BF16)

    sums = jnp.sum(hid_rows[...].astype(F32) * q[...], axis=1, keepdims=True)
    spread = jnp.where(
        iota((rows, LANES), 1) == iota((rows, LANES), 0) % WIDE, sums, 0.0
    ).reshape(n, 2, WIDE, LANES)
    spread = jnp.sum(spread, axis=2)
    part_out[...] = spread[:, 1]
    part_copy = remote(part_out, part_in, part_ssem, part_rsem, (da, e))
    part_copy.start()
    hg_send[...] = weigh(1)
    hg_copy.start()
    hg_own[...] = weigh(0)
    hg_store.start()
    part_copy.wait_recv()
    total = spread[:, 0] + part_in[...]
    back_out[...] = jnp.broadcast_to(total[:, None, :], (n, 8, LANES))

    def give(j, carry):
        to = (e + j) % (2 * n)
        remote(
            back_out.at[to % n], back_in.at[e], back_ssem, back_rsem, (d, to)
        ).start()
        return carry

    lax.fori_loop(1, 2 * n, give, 0)
    back_in[e] = back_out[i]
    many = pl.ds(0, 2 * n - 1)
    remote(back_in.at[many], back_in.at[many], back_ssem, back_rsem, (db, e)).wait()
    table = back_in[...][:, 0, :]
    own_rows_in = pl.ds(own_block, tokens)
    base = plane - (zl * cap).astype(F32)
    for k, place in enumerate((place0, place1)):
        at = place[own_rows_in, :] + base
        name = jnp.floor((at + 0.5) / span)
        member = (lane_f == name).astype(F32)
        slot = (at - name * span)[:, 0:1]
        found = jnp.dot(
            member[:, : 2 * n], table, preferred_element_type=F32, precision=lax.Precision.HIGHEST
        )
        at = slot + (zl * cap).astype(F32)
        value = jnp.sum(jnp.where(lane_f == at, found, 0.0), axis=1, keepdims=True)
        prob_ref[:, k : k + 1] = value

    for k in range(chunks):
        end_tokens(k)
        w_copies[k].wait_send()
        row_wait(k).wait_send()
        dg_copies[k].wait()
        own_copies[k].wait()
    for copy in meta_copies:
        copy.wait_send()
    hid_copy.wait_send()
    part_copy.wait_send()
    hg_copy.wait()
    hg_store.wait()


def per_device(grad_out, routes, route_weight, hidden_saved, down_weight):
    tokens, width = grad_out.shape
    n = lax.axis_size("expert") // 2
    cap, hidden_width = hidden_saved.shape[3], hidden_saved.shape[4]
    quarter = down_weight.shape[1]
    half = 2 * quarter
    chunks = 7
    chunk = width // chunks
    rows = n * 2 * WIDE
    slots = 2 * n * cap
    hidden = hidden_saved.reshape(2 * n, cap, hidden_width).transpose(1, 0, 2)
    vmem = pl.BlockSpec(memory_space=pltpu.VMEM)
    anywhere = pl.BlockSpec(memory_space=pl.ANY)
    sem = pltpu.SemaphoreType.DMA
    flops = 2 * rows * width * (4 * tokens + half + half)
    own, other, hidden_grad, prob_grad = pl.pallas_call(
        functools.partial(kernel, n, cap, tokens, chunk, chunks, quarter),
        out_shape=(
            jax.ShapeDtypeStruct((quarter, width), F32),
            jax.ShapeDtypeStruct((quarter, width), BF16),
            jax.ShapeDtypeStruct((slots, hidden_width), BF16),
            jax.ShapeDtypeStruct((tokens, 2), F32),
        ),
        in_specs=[anywhere, vmem, vmem, anywhere, anywhere],
        out_specs=(anywhere, anywhere, anywhere, vmem),
        scratch_shapes=[
            pltpu.VMEM((chunks, 4 * tokens, chunk), BF16),
            pltpu.VMEM((4, 16, 256), BF16),
            pltpu.VMEM((4 * tokens, LANES), F32),
            pltpu.VMEM((4 * tokens, LANES), F32),
            pltpu.VMEM((4 * tokens, LANES), BF16),
            pltpu.VMEM((4 * tokens, LANES), BF16),
            pltpu.VMEM((rows, 4 * tokens), BF16),
            pltpu.VMEM((slots, n * WIDE), BF16),
            pltpu.VMEM((rows, chunk + LANES), BF16),
            pltpu.VMEM((rows, chunk + LANES), BF16),
            pltpu.VMEM((chunks - 1, rows, chunk), BF16),
            pltpu.VMEM((chunks - 1, rows, chunk), BF16),
            pltpu.VMEM((chunks, half, chunk), BF16),
            pltpu.VMEM((slots, hidden_width), BF16),
            pltpu.VMEM((slots, half), BF16),
            pltpu.VMEM((rows, half), BF16),
            pltpu.VMEM((half, rows), BF16),
            pltpu.VMEM((rows, half), F32),
            pltpu.VMEM((chunks, quarter, chunk), F32),
            pltpu.VMEM((chunks, quarter, chunk), BF16),
            pltpu.VMEM((slots, half), BF16),
            pltpu.VMEM((slots, half), BF16),
            pltpu.VMEM((n, LANES), F32),
            pltpu.VMEM((n, LANES), F32),
            pltpu.VMEM((n, 8, LANES), F32),
            pltpu.VMEM((2 * n, 8, LANES), F32),
            sem((2 * chunks + 1,)),
            sem((chunks, 3)),
            sem((chunks, 4)),
            sem((3,)),
            sem((3,)),
            sem,
            sem,
            sem((chunks,)),
            sem((chunks,)),
            sem((chunks,)),
            sem((chunks,)),
            sem((chunks,)),
            sem((chunks,)),
            sem((chunks + 1,)),
            sem,
            sem,
            sem,
            sem,
            sem,
            sem,
        ],
        compiler_params=pltpu.CompilerParams(
            collective_id=0, has_side_effects=True, vmem_limit_bytes=62 * 1024 * 1024
        ),
        cost_estimate=pl.CostEstimate(flops=flops, bytes_accessed=1 << 24, transcendentals=0),
    )(
        grad_out,
        routes.T,
        route_weight.T,
        hidden.reshape(slots, hidden_width),
        down_weight.reshape(quarter, width),
    )
    down_grad = own + other.astype(F32)
    hidden_grad = hidden_grad.reshape(cap, 2 * n, hidden_width).transpose(1, 0, 2)
    return (
        down_grad.reshape(1, quarter, width),
        hidden_grad.reshape(hidden_saved.shape),
        prob_grad,
    )


def solution(mesh):
    placed = (
        P(("dp", "expert"), None),
        P(("dp", "expert"), None),
        P(("dp", "expert"), None),
        P("expert", "dp", None, None, None),
        P("expert", "dp", None),
    )
    return jax.shard_map(
        per_device,
        mesh=mesh,
        in_specs=placed,
        out_specs=(
            P("expert", "dp", None),
            P("expert", "dp", None, None, None),
            P(("dp", "expert"), None),
        ),
        check_vma=False,
    )
```
